128 devices in a mesh: dp: 8 (over x_lo, z), tp: 16 (over x_hi, y, core).
Axes of the slice: x: 4 (x_hi: 2, x_lo: 2; x = x_hi * 2 + x_lo), y: 4, z: 4, core: 2. Of those that a mesh axis runs over, the one named last changes fastest.
Arguments:
- queries: bfloat16 [1024, 8192], P('dp', 'tp'), may hold values from -160 to 160
- keys_cache: bfloat16 [256, 16, 384, 128], P('dp', 'tp'), may hold values from -7 to 7, as said below
- values_cache: bfloat16 [256, 16, 384, 128], P('dp', 'tp'), may hold values from -6 to 6, as said below
- prefix_len: int32 [256], P('dp'), may hold values from 2 to 380, as said below
- accepted: int32 [256], P('dp'), may hold values from 1 to 4
- residual_in: bfloat16 [1024, 8192], P('dp', 'tp'), may hold values from -0.59765625 to 0.59765625
- low_hidden: bfloat16 [1024, 8192], P('dp', 'tp'), may hold values from -6 to 6
- mid_hidden: bfloat16 [1024, 8192], P('dp', 'tp'), may hold values from -6 to 6
- out_weight: bfloat16 [8192, 8192], P('tp'), may hold values from -0.0625 to 0.0625
- merge_weight: bfloat16 [3, 8192, 8192], P(None, 'dp', 'tp'), may hold values from -0.0390625 to 0.0390625
Outputs:
- top_hidden: bfloat16 [1024, 8192], P('dp', 'tp')
- merge_grad: float32 [3, 8192, 8192], P(None, 'dp', 'tp')
The draws below stay inside these ranges and needn't reach their ends.
Inputs may be any that keep to these rules, and one draw needn't show every extreme that they name: Slots j and i of keys_cache hold the same key head k, and are equal, when j * 8 // 16 = i * 8 // 16 = k. Slots j and i of values_cache hold the same value head k, and are equal, when j * 8 // 16 = i * 8 // 16 = k. `prefix_len`: some row has the largest length.
All inputs are finite; a program needn't handle non-finite values.
Results may differ from the reference program's by a relative error of at most 0.014.
Values may be sent and summed in bfloat16 or wider, within the bound.
No kernel may reach another device: no remote copies, remote signals or barrier semaphores. Data moves between devices by JAX's collectives and lax.ppermute only.
A program may use at most 128 MiB of HBM per device.

```python
import jax
import jax.numpy as jnp
from jax import lax

D = 8192
HEADS = 64
KVH = 8
HD = 128
STEPS = 4
CACHE = 384
ROWS = 256
TOKENS = 1024
N_TP = 16


def shared_keys(key):
    base = jax.random.normal(key, (ROWS, KVH, CACHE, HD), jnp.float32)
    return jnp.clip(base, -6.0, 6.0)


def draw_keys_cache(key, part):
    base = shared_keys(key)
    return jnp.repeat(base, N_TP // KVH, axis=1).astype(jnp.bfloat16)


def draw_queries(key, part):
    key = jax.random.fold_in(key, 12)
    first_key = jax.random.fold_in(key, 0)
    drawn = jnp.clip(jax.random.normal(first_key, (ROWS, STEPS, HEADS, HD), jnp.float32), -6.0, 6.0)
    return drawn.reshape(ROWS * STEPS, HEADS * HD).astype(jnp.bfloat16)


def draw_values_cache(key, part):
    key = jax.random.fold_in(key, 13)
    base = jnp.clip(jax.random.normal(key, (ROWS, KVH, CACHE, HD), jnp.float32), -6.0, 6.0)
    return jnp.repeat(base, N_TP // KVH, axis=1).astype(jnp.bfloat16)


def draw_prefix_len(key, part):
    key = jax.random.fold_in(key, 14)
    first_key, second_key = jax.random.split(key)
    lengths = jax.random.randint(first_key, (ROWS,), 2, CACHE - STEPS + 1, jnp.int32)
    where_row = jax.random.randint(second_key, (), 0, ROWS, jnp.int32)
    return lengths.at[where_row].set(CACHE - STEPS)


def plant(drawn, stream_key, smallest, largest):
    longest = drawn.shape.index(max(drawn.shape))
    spots = []
    for shift in (0, 1):
        where = [jax.random.randint(jax.random.fold_in(stream_key, axis), (), 0, length) for axis, length in enumerate(drawn.shape)]
        where[longest] = (where[longest] + shift) % drawn.shape[longest]
        spots.append(tuple(where))
    return drawn.at[spots[0]].set(smallest).at[spots[1]].set(largest)


def levels(key, shape, cuts, smallest, largest):
    def one(axis_at, blocks):
        steps = jax.random.uniform(jax.random.fold_in(jax.random.fold_in(key, 6), axis_at), (blocks,), jnp.float32, smallest / len(cuts), largest / len(cuts))
        return jnp.repeat(jnp.exp(steps), shape[axis_at] // blocks).reshape((-1,) + (1,) * (len(shape) - axis_at - 1))

    loudness = one(*cuts[0])
    for cut in cuts[1:]:
        loudness = loudness * one(*cut)
    return loudness


def scatter_about(rng, shape, spread, most, shards=(), kind=jnp.bfloat16):
    result = jax.random.normal(rng, shape, jnp.float32) * spread
    if len(shards) > 0:
        result = levels(rng, shape, shards, -0.22, 0.18) * result
    return jnp.clip(result, min=-most, max=most).astype(kind)


def setup_inputs(seed: int = 0) -> dict:
    streams_of = jax.random.split(jax.random.key(seed), 11)
    return {
        "queries": draw_queries(jax.random.fold_in(streams_of[10], 71), 0),
        "keys_cache": draw_keys_cache(jax.random.fold_in(streams_of[10], 71), 0),
        "values_cache": draw_values_cache(jax.random.fold_in(streams_of[10], 71), 0),
        "prefix_len": draw_prefix_len(jax.random.fold_in(streams_of[10], 71), 0),
        "accepted": plant(jax.random.randint(streams_of[4], (ROWS,), 1, STEPS + 1), jax.random.fold_in(streams_of[4], 1), 1, STEPS).astype(jnp.int32),
        "residual_in": scatter_about(streams_of[5], (TOKENS, D), 0.1, 0.59765625, ((0, 8), (1, 16))),
        "low_hidden": scatter_about(streams_of[6], (TOKENS, D), 1.0, 6.0, ((0, 8), (1, 16))),
        "mid_hidden": scatter_about(streams_of[7], (TOKENS, D), 1.0, 6.0, ((0, 8), (1, 16))),
        "out_weight": scatter_about(streams_of[8], (HEADS * HD, D), (HEADS * HD) ** -0.5, 0.0625, ((0, 16),)),
        "merge_weight": scatter_about(streams_of[9], (3, D, D), (3 * D) ** -0.5, 0.0390625, ((1, 8), (2, 16))),
    }


def attend(q, k, v, lens):
    scores = jnp.einsum('rshd,rpd->rhsp', q.astype(jnp.float32), k.astype(jnp.float32)) * (HD ** -0.5)
    limit = lens[:, None] + jnp.arange(q.shape[1], dtype=jnp.int32)[None, :] + 1
    visible = jnp.arange(k.shape[1], dtype=jnp.int32)[None, None, :] < limit[:, :, None]
    scores = jnp.where(visible[:, None], scores, -1e30)
    top = jnp.max(scores, axis=-1, keepdims=True)
    expo = jnp.exp(scores - top)
    weights = (expo / jnp.sum(expo, axis=-1, keepdims=True)).astype(jnp.bfloat16)
    context = jnp.einsum('rhsp,rpd->rshd', weights.astype(jnp.float32), v.astype(jnp.float32))
    return context.astype(jnp.bfloat16)


def reference(queries, keys_cache, values_cache, prefix_len, accepted, residual_in, low_hidden, mid_hidden, out_weight, merge_weight):
    per_slot = HEADS // N_TP
    grouped = queries.reshape(ROWS, STEPS, N_TP, per_slot, HD)
    grouped = jnp.moveaxis(grouped, 2, 0)
    keys_slot = jnp.moveaxis(keys_cache, 1, 0)
    values_slot = jnp.moveaxis(values_cache, 1, 0)

    def one_slot(items):
        return attend(items[0], items[1], items[2], prefix_len)

    context = lax.map(one_slot, (grouped, keys_slot, values_slot))
    context = jnp.moveaxis(context, 0, 2).reshape(TOKENS, HEADS * HD)
    projected = jnp.dot(context, out_weight, preferred_element_type=jnp.float32)
    top_hidden = (residual_in.astype(jnp.float32) + projected).astype(jnp.bfloat16)
    merged = jnp.dot(low_hidden, merge_weight[0], preferred_element_type=jnp.float32)
    merged = merged + jnp.dot(mid_hidden, merge_weight[1], preferred_element_type=jnp.float32)
    merged = merged + jnp.dot(top_hidden, merge_weight[2], preferred_element_type=jnp.float32)
    rows3 = top_hidden.reshape(ROWS, STEPS, D)
    following = jnp.concatenate([rows3[:, 1:], jnp.zeros_like(rows3[:, :1])], axis=1).reshape(TOKENS, D)
    keep = ((jnp.arange(STEPS, dtype=jnp.int32)[None, :] + 1) < accepted[:, None]).astype(jnp.float32).reshape(TOKENS)
    errors = (keep[:, None] * (merged - following.astype(jnp.float32)) * (TOKENS ** -0.5)).astype(jnp.bfloat16)
    grads = []
    for source in (low_hidden, mid_hidden, top_hidden):
        grads.append(lax.dot_general(source, errors, (((0,), (0,)), ((), ())), preferred_element_type=jnp.float32))
    return top_hidden, jnp.stack(grads, axis=0)
```

```python
import jax
import jax.numpy as jnp
from jax import lax
from jax.sharding import PartitionSpec as P

STEPS = 4
CHIPS = 8


def dev(xl, z, xh, y, c):
    return (xl * 4 + z) * 16 + xh * 8 + y * 2 + c


def coords():
    return [
        (xl, z, xh, y, c)
        for xl in range(2)
        for z in range(4)
        for xh in range(2)
        for y in range(4)
        for c in range(2)
    ]


TO_READER = [(dev(*p), dev(p[2], p[3], p[0], (p[3] - p[1]) % 4, p[4])) for p in coords()]
READERS = [
    [dev(xl, z, xh, (z - k) % 4, c) for xh in range(2) for k in range(4)]
    for xl in range(2)
    for z in range(4)
    for c in range(2)
]
READERS_BOTH = [
    [dev(xl, z, xh, (z - k) % 4, c) for c in range(2) for xh in range(2) for k in range(4)]
    for xl in range(2)
    for z in range(4)
]
SAME_CORE = [[2 * t + c for t in range(CHIPS)] for c in range(2)]
OTHER_CORE = [(j, j ^ 1) for j in range(16)]
BOTH = ("dp", "tp")


def attend(queries, keys, values, lens):
    rows = keys.shape[0]
    head_size = keys.shape[-1]
    grouped = queries.reshape(rows, STEPS, -1, head_size)
    scores = jnp.einsum(
        "rshd,rpd->rhsp", grouped, keys, preferred_element_type=jnp.float32
    ) * head_size ** (-0.5)
    limit = lens[:, None] + jnp.arange(STEPS, dtype=jnp.int32)[None, :] + 1
    visible = jnp.arange(keys.shape[1], dtype=jnp.int32)[None, None, :] < limit[:, :, None]
    scores = jnp.where(visible[:, None], scores, -1e30)
    largest = jnp.max(scores, axis=-1, keepdims=True)
    expo = jnp.exp(scores - largest)
    weights = (expo / jnp.sum(expo, axis=-1, keepdims=True)).astype(jnp.bfloat16)
    context = jnp.einsum("rhsp,rpd->rshd", weights, values, preferred_element_type=jnp.float32)
    return context.astype(jnp.bfloat16).reshape(rows * STEPS, -1)


def dot(a, b):
    return jnp.dot(a, b, preferred_element_type=jnp.float32)


def contract(source, errors):
    return lax.dot_general(
        source, errors, (((0,), (0,)), ((), ())), preferred_element_type=jnp.float32
    )


def spread(block, axis, groups=None):
    copies = jnp.broadcast_to(block[None], (CHIPS, *block.shape))
    return lax.all_to_all(copies, axis, 0, 0, tiled=True, axis_index_groups=groups)


def local(
    queries,
    keys_cache,
    values_cache,
    prefix_len,
    accepted,
    residual_in,
    low_hidden,
    mid_hidden,
    out_weight,
    merge_weight,
):
    tokens, width = residual_in.shape
    core = lax.axis_index("tp") % 2

    both = lax.ppermute(jnp.concatenate([low_hidden, mid_hidden], axis=1), BOTH, TO_READER)
    both = lax.all_gather(both, BOTH, axis=0, tiled=True, axis_index_groups=READERS_BOTH)
    both = both.reshape(2, CHIPS * tokens, 2 * width)
    weight = merge_weight.reshape(3, 2, width, width)
    merged_both = dot(both[0], weight[:2, 0].reshape(2 * width, width)) + dot(
        both[1], weight[:2, 1].reshape(2 * width, width)
    )
    weight_own = lax.dynamic_index_in_dim(weight[2], core, 0, keepdims=False)
    weight_other = lax.dynamic_index_in_dim(weight[2], 1 - core, 0, keepdims=False)

    context = attend(queries, keys_cache[:, 0], values_cache[:, 0], prefix_len)
    projected = dot(context, out_weight).astype(jnp.bfloat16)
    projected = projected.reshape(tokens, CHIPS, 2, width).transpose(2, 1, 0, 3)
    kept = lax.dynamic_index_in_dim(projected, core, 0, keepdims=False)
    given = lax.dynamic_index_in_dim(projected, 1 - core, 0, keepdims=False)
    taken = lax.ppermute(given, "tp", OTHER_CORE)
    pair = (kept.astype(jnp.float32) + taken.astype(jnp.float32)).astype(jnp.bfloat16)
    parts = lax.all_to_all(pair, "tp", 0, 0, tiled=True, axis_index_groups=SAME_CORE)
    summed = jnp.sum(parts.astype(jnp.float32), axis=0)
    top_hidden = (residual_in.astype(jnp.float32) + summed).astype(jnp.bfloat16)

    top_own = spread(lax.ppermute(top_hidden, BOTH, TO_READER), BOTH, READERS)
    top_other = lax.ppermute(top_own, "tp", OTHER_CORE)
    top_own = top_own.reshape(CHIPS * tokens, width)
    top_other = top_other.reshape(CHIPS * tokens, width)

    merged_part = merged_both + dot(top_own, weight_own) + dot(top_other, weight_other)
    merged_part = merged_part.astype(jnp.bfloat16).reshape(CHIPS, tokens, width)
    merged_parts = lax.all_to_all(merged_part, "dp", 0, 0, tiled=True)
    merged = jnp.sum(merged_parts.astype(jnp.float32), axis=0)

    step = lax.broadcasted_iota(jnp.int32, (tokens, 1), 0) % STEPS
    keep = (step + 1 < jnp.repeat(accepted, STEPS)[:, None]).astype(jnp.float32)
    following = jnp.concatenate([top_hidden[1:], jnp.zeros_like(top_hidden[:1])], axis=0)
    following = jnp.where(step < STEPS - 1, following, jnp.zeros_like(following))
    scale = (CHIPS * tokens) ** (-0.5)
    errors = (keep * (merged - following.astype(jnp.float32)) * scale).astype(jnp.bfloat16)
    errors = spread(errors, "dp").reshape(CHIPS * tokens, width)

    grad_both = [contract(both[half], errors).reshape(2, width, width) for half in range(2)]
    grad_own, grad_other = contract(top_own, errors), contract(top_other, errors)
    grad_top = jnp.where(
        core == 0, jnp.stack([grad_own, grad_other]), jnp.stack([grad_other, grad_own])
    )
    grad = jnp.concatenate([jnp.stack(grad_both, axis=1), grad_top[None]], axis=0)
    return (top_hidden, grad.reshape(3, 2 * width, width))


def solution(mesh):
    in_specs = (
        P("dp", "tp"),
        P("dp", "tp", None, None),
        P("dp", "tp", None, None),
        P("dp"),
        P("dp"),
        P("dp", "tp"),
        P("dp", "tp"),
        P("dp", "tp"),
        P("tp", None),
        P(None, "dp", "tp"),
    )
    out_specs = (P("dp", "tp"), P(None, "dp", "tp"))
    return jax.shard_map(local, mesh=mesh, in_specs=in_specs, out_specs=out_specs, check_vma=False)
```

```python
import functools

import jax
import jax.numpy as jnp
from jax import lax
from jax.experimental import pallas as pl
from jax.experimental.pallas import tpu as pltpu
from jax.sharding import PartitionSpec as P

STEPS = 4
CHIPS = 8
VMEM = 62 * 2**20


def dev(xl, z, xh, y, c):
    return (xl * 4 + z) * 16 + xh * 8 + y * 2 + c


def coords():
    return [
        (xl, z, xh, y, c)
        for xl in range(2)
        for z in range(4)
        for xh in range(2)
        for y in range(4)
        for c in range(2)
    ]


TO_READER = [(dev(*p), dev(p[2], p[3], p[0], (p[3] - p[1]) % 4, p[4])) for p in coords()]
TO_ACROSS = [(dev(*p), dev(p[2], p[3], 1 - p[0], (p[3] - p[1]) % 4, p[4])) for p in coords()]
READERS = [
    [dev(xl, z, xh, (z - k) % 4, c) for xh in range(2) for k in range(4)]
    for xl in range(2)
    for z in range(4)
    for c in range(2)
]
SAME_CORE = [[2 * t + c for t in range(CHIPS)] for c in range(2)]
OTHER_CORE = [(j, j ^ 1) for j in range(16)]
BOTH = ("dp", "tp")
SCALARS = pl.BlockSpec(memory_space=pltpu.SMEM)
HERE = pl.BlockSpec(memory_space=pltpu.VMEM)
THERE = pl.BlockSpec(memory_space=pl.ANY)
FREE = pl.CostEstimate(flops=0, bytes_accessed=0, transcendentals=0)


def from_y(far):
    return [(j, (j & 8) | (j - 2 * far) % 8) for j in range(16)]


def dot(a, b):
    return jnp.dot(a, b, preferred_element_type=jnp.float32)


def spread(block, axis, groups=None):
    copies = jnp.broadcast_to(block[None], (CHIPS, *block.shape))
    return lax.all_to_all(copies, axis, 0, 0, tiled=True, axis_index_groups=groups)


def fetch(pairs, sems):
    copies = [
        pltpu.make_async_copy(source, target, sems.at[i])
        for i, (source, target) in enumerate(pairs)
    ]
    for copy in copies:
        copy.start()
    return copies


def attend_kernel(lens, queries, keys, values, out, held, scores, weights, gathered, sems):
    rows, width = held.shape[1], keys.shape[2]
    heads = queries.shape[1] // width
    size = heads * STEPS
    copies = fetch(
        [
            (source.at[pl.ds(i * rows // 2, rows // 2)], held.at[j, pl.ds(i * rows // 2, rows // 2)])
            for i in range(2)
            for j, source in enumerate((keys, values))
        ],
        sems,
    )
    shape = (size, keys.shape[1])
    position = lax.broadcasted_iota(jnp.int32, shape, 1)
    step = lax.broadcasted_iota(jnp.int32, shape, 0) % STEPS
    scale = width ** (-0.5)
    for h in range(heads):
        asked = queries[:, h * width : (h + 1) * width].astype(jnp.float32)
        for r in range(rows):
            gathered[r, h * STEPS : (h + 1) * STEPS, :] = asked[r * STEPS : (r + 1) * STEPS]
    for i in range(2):
        copies[2 * i].wait()
        for r in range(i * rows // 2, (i + 1) * rows // 2):
            score = lax.dot_general(
                gathered[r].astype(queries.dtype), held[0, r], (((1,), (1,)), ((), ())), preferred_element_type=jnp.float32
            )
            visible = position < lens[r] + step + 1
            scores[r * size : (r + 1) * size, :] = jnp.where(visible, score * scale, -1e30)
        part = slice(i * rows * size // 2, (i + 1) * rows * size // 2)
        score = scores[part, :]
        expo = jnp.exp(score - jnp.max(score, axis=-1, keepdims=True))
        inverse = 1.0 / jnp.sum(expo, axis=-1, keepdims=True)
        weights[part, :] = (expo * inverse).astype(weights.dtype)
        copies[2 * i + 1].wait()
        for r in range(i * rows // 2, (i + 1) * rows // 2):
            gathered[r] = dot(weights[r * size : (r + 1) * size, :], held[1, r])
    for h in range(heads):
        context = [gathered[r, h * STEPS : (h + 1) * STEPS, :] for r in range(rows)]
        out[:, h * width : (h + 1) * width] = jnp.concatenate(context, axis=0).astype(out.dtype)


def attend(queries, keys, values, lens):
    rows, positions, width = keys.shape
    tokens, depth = queries.shape
    size = STEPS * depth // width
    return pl.pallas_call(
        attend_kernel,
        in_specs=[SCALARS, HERE, THERE, THERE],
        out_specs=HERE,
        out_shape=jax.ShapeDtypeStruct(queries.shape, queries.dtype),
        scratch_shapes=[
            pltpu.VMEM((2, rows, positions, width), jnp.bfloat16),
            pltpu.VMEM((rows * size, positions), jnp.float32),
            pltpu.VMEM((rows * size, positions), jnp.bfloat16),
            pltpu.VMEM((rows, size, width), jnp.float32),
            pltpu.SemaphoreType.DMA((4,)),
        ],
        compiler_params=pltpu.CompilerParams(vmem_limit_bytes=VMEM),
        cost_estimate=FREE,
        name="attend",
    )(lens, queries, keys, values)


def pack_kernel(cuts, *refs):
    *sources, out, held, in_sems, out_sem = refs
    for copy in fetch([(s, held.at[cut]) for s, cut in zip(sources, cuts)], in_sems):
        copy.wait()
    for copy in fetch([(held, out)], out_sem):
        copy.wait()


def pack(arrays, axis):
    shape = list(arrays[0].shape)
    size = shape[axis]
    cuts = [(slice(None),) * axis + (slice(i * size, (i + 1) * size),) for i in range(len(arrays))]
    shape[axis] *= len(arrays)
    return pl.pallas_call(
        functools.partial(pack_kernel, cuts),
        in_specs=[THERE] * len(arrays),
        out_specs=THERE,
        out_shape=jax.ShapeDtypeStruct(shape, arrays[0].dtype),
        scratch_shapes=[
            pltpu.VMEM(shape, arrays[0].dtype),
            pltpu.SemaphoreType.DMA((len(arrays),)),
            pltpu.SemaphoreType.DMA((1,)),
        ],
        compiler_params=pltpu.CompilerParams(vmem_limit_bytes=VMEM),
        cost_estimate=FREE,
        name="pack",
    )(*arrays)


def project_kernel(half, context, weight, out, held, sems):
    width = out.shape[-1]
    copies = fetch(
        [
            (weight.at[:, pl.ds((2 * t + half[0]) * width, width)], held.at[t])
            for t in range(CHIPS)
        ],
        sems,
    )
    for t in range(CHIPS):
        copies[t].wait()
        out[t] = dot(context[...], held[t]).astype(out.dtype)


def project(context, weight, half):
    tokens, depth = context.shape
    width = weight.shape[1] // (2 * CHIPS)
    return pl.pallas_call(
        project_kernel,
        in_specs=[SCALARS, HERE, THERE],
        out_specs=HERE,
        out_shape=jax.ShapeDtypeStruct((CHIPS, tokens, width), jnp.bfloat16),
        scratch_shapes=[
            pltpu.VMEM((CHIPS, depth, width), jnp.bfloat16),
            pltpu.SemaphoreType.DMA((CHIPS,)),
        ],
        compiler_params=pltpu.CompilerParams(vmem_limit_bytes=VMEM),
        cost_estimate=FREE,
        name="project",
    )(half, context, weight)


def base_kernel(core, *refs):
    count = len(refs) - 5
    sources, (weight, out, held, held_weight, sems) = refs[:count], refs[count:]
    copies = fetch(
        [(weight.at[k], held_weight.at[k]) for k in range(2)]
        + [(source, held.at[i]) for i, source in enumerate(sources)],
        sems,
    )
    half = core[0]
    width = out.shape[-1]
    rows = sources[0].shape[0]
    copies[0].wait()
    copies[1].wait()
    for i in range(count // 2):
        copies[2 + 2 * i].wait()
        copies[3 + 2 * i].wait()
        total = dot(held[2 * i, :, :width], held_weight[0, half])
        total += dot(held[2 * i, :, width:], held_weight[1, half])
        total += dot(held[2 * i + 1, :, :width], held_weight[0, 1 - half])
        total += dot(held[2 * i + 1, :, width:], held_weight[1, 1 - half])
        out[i * rows : (i + 1) * rows, :] = total.astype(out.dtype)


def base(pieces, weight, core):
    rows, depth = pieces[0].shape
    tokens, width = len(pieces) // 2 * rows, depth // 2
    return pl.pallas_call(
        base_kernel,
        in_specs=[SCALARS] + [THERE] * (len(pieces) + 1),
        out_specs=HERE,
        out_shape=jax.ShapeDtypeStruct((tokens, width), jnp.bfloat16),
        scratch_shapes=[
            pltpu.VMEM((len(pieces), rows, depth), jnp.bfloat16),
            pltpu.VMEM((2, *weight.shape[1:]), jnp.bfloat16),
            pltpu.SemaphoreType.DMA((len(pieces) + 2,)),
        ],
        compiler_params=pltpu.CompilerParams(vmem_limit_bytes=VMEM),
        cost_estimate=FREE,
        name="base",
    )(core, *pieces, weight)


def add_kernel(own, core, places, total, source, weight, out, held, near, held_weight, sems):
    blocks, rows, width = source.shape
    half = core[0] if own else 1 - core[0]
    pairs = [(weight.at[2, half], held_weight)]
    for p in range(0, blocks, 2):
        pairs.append((source.at[p : p + 2], near.at[p : p + 2]))
        pairs += [(total.at[places[i] if own else i], held.at[i]) for i in (p, p + 1)]
    copies = fetch(pairs, sems)
    copies[0].wait()
    for p in range(0, blocks, 2):
        for copy in copies[1 + p // 2 * 3 : 4 + p // 2 * 3]:
            copy.wait()
        added = dot(near[p : p + 2].reshape(2 * rows, width), held_weight[...])
        added = added.reshape(2, rows, width) + held[p : p + 2].astype(jnp.float32)
        out[p : p + 2] = added.astype(out.dtype)


def add_top(own, total, source, weight, core, places):
    blocks, rows, width = total.shape
    return pl.pallas_call(
        functools.partial(add_kernel, own),
        in_specs=[SCALARS] * 2 + [THERE] * 3,
        out_specs=HERE,
        out_shape=jax.ShapeDtypeStruct(total.shape, total.dtype),
        scratch_shapes=[
            pltpu.VMEM(total.shape, total.dtype),
            pltpu.VMEM(source.shape, source.dtype),
            pltpu.VMEM(weight.shape[2:], weight.dtype),
            pltpu.SemaphoreType.DMA((1 + blocks // 2 * 3,)),
        ],
        compiler_params=pltpu.CompilerParams(vmem_limit_bytes=VMEM),
        cost_estimate=FREE,
        name="add_top",
    )(core, places, total, source, weight)


def grad_kernel(core, places, errors, *refs):
    count = len(refs) - 10
    pieces, (top_own, top_other, out, near, ordered, held, tops, made, sems, out_sems) = (
        refs[:count],
        refs[count:],
    )
    blocks, rows, width = errors.shape
    tokens = blocks * rows
    pairs = [(errors, near)]
    pairs += [(pieces[i], held.at[0, i // 2]) for i in range(0, count, 2)]
    first = fetch(pairs, sems)
    rest = [(pieces[i], held.at[1, i // 2]) for i in range(1, count, 2)]
    rest += [(top_own, tops.at[0]), (top_other, tops.at[1])]

    def product(source, target):
        return lax.dot_general(
            source, target, (((0,), (0,)), ((), ())), preferred_element_type=jnp.float32
        )

    first[0].wait()
    for p in range(blocks):
        ordered[p * rows : (p + 1) * rows, :] = near[places[p]]
    for copy in first[1:]:
        copy.wait()
    rest = fetch(rest, sems.at[pl.ds(len(pairs), len(rest))])
    sent = []
    for i in range(6):
        if i == 2:
            for copy in rest[: count // 2]:
                copy.wait()
        if i >= 4:
            rest[count // 2 + i - 4].wait()
        half = 1 - core[0] if i in (2, 3, 5) else core[0]
        for part in range(2):
            step, cut = 2 * i + part, width // 2
            slot = step % made.shape[0]
            if step >= made.shape[0]:
                sent[step - made.shape[0]].wait()
            columns = slice(part * cut, (part + 1) * cut)
            if i < 4:
                columns = slice(i % 2 * width + part * cut, i % 2 * width + (part + 1) * cut)
                source = held[i // 2, :, :, columns].reshape(tokens, cut)
                made[slot] = product(source, ordered[...])
            else:
                made[slot] = product(tops[i - 4, :, columns], near[...].reshape(tokens, width))
            target = out.at[i % 2 if i < 4 else 2, pl.ds(half * width + part * cut, cut)]
            copy = pltpu.make_async_copy(made.at[slot], target, out_sems.at[step])
            copy.start()
            sent.append(copy)
    for copy in sent[-made.shape[0] :]:
        copy.wait()


def grad(errors, pieces, top_own, top_other, core, places):
    blocks, rows, width = errors.shape
    tokens = blocks * rows
    count = len(pieces)
    return pl.pallas_call(
        grad_kernel,
        in_specs=[SCALARS] * 2 + [THERE] * (count + 3),
        out_specs=THERE,
        out_shape=jax.ShapeDtypeStruct((3, 2 * width, width), jnp.float32),
        scratch_shapes=[
            pltpu.VMEM(errors.shape, jnp.bfloat16),
            pltpu.VMEM((tokens, width), jnp.bfloat16),
            pltpu.VMEM((2, count // 2, *pieces[0].shape), jnp.bfloat16),
            pltpu.VMEM((2, tokens, width), jnp.bfloat16),
            pltpu.VMEM((4, width // 2, width), jnp.float32),
            pltpu.SemaphoreType.DMA((count + 3,)),
            pltpu.SemaphoreType.DMA((12,)),
        ],
        compiler_params=pltpu.CompilerParams(vmem_limit_bytes=VMEM),
        cost_estimate=FREE,
        name="grad",
    )(core, places, errors, *pieces, top_own, top_other)


def local(
    queries,
    keys_cache,
    values_cache,
    prefix_len,
    accepted,
    residual_in,
    low_hidden,
    mid_hidden,
    out_weight,
    merge_weight,
):
    tokens, width = residual_in.shape
    me_dp, me_tp = lax.axis_index("dp"), lax.axis_index("tp")
    xl, z = me_dp // 4, me_dp % 4
    xh, y, core = me_tp // 8, me_tp // 2 % 4, me_tp % 2
    me = core.reshape(1)
    index = jnp.arange(CHIPS)
    lies = ((z - y - index) % 4 * 2 + (xh ^ (index // 4))).astype(jnp.int32)
    held = ((xh ^ (index % 2)) * 4 + (z - y - index // 2) % 4).astype(jnp.int32)
    weight = merge_weight.reshape(3, 2, width, width)

    both = pack([low_hidden, mid_hidden], 1)
    both = [lax.ppermute(both, BOTH, way) for way in (TO_READER, TO_ACROSS)]
    context = attend(queries, keys_cache[:, 0], values_cache[:, 0], prefix_len)
    taken = project(context, out_weight, 1 - me)
    taken, *both = lax.optimization_barrier((taken, *both))
    both = pack(both, 0)
    both = [both] + [lax.ppermute(both, "tp", from_y(far)) for far in (1, 2, 3)]
    taken = lax.ppermute(taken, "tp", OTHER_CORE)
    kept = project(context, out_weight, me)
    pair = (kept.astype(jnp.float32) + taken.astype(jnp.float32)).astype(jnp.bfloat16)
    pair, *both = lax.optimization_barrier((pair, *both))
    parts = lax.all_to_all(pair, "tp", 0, 0, tiled=True, axis_index_groups=SAME_CORE)
    summed = jnp.sum(parts.astype(jnp.float32), axis=0)
    top_hidden = (residual_in.astype(jnp.float32) + summed).astype(jnp.bfloat16)

    pieces = []
    for piece in both:
        pieces += [piece, lax.ppermute(piece, "tp", OTHER_CORE)]
    total = base(pieces, weight, me).reshape(CHIPS, tokens, width)
    top_hidden, total = lax.optimization_barrier((top_hidden, total))

    top_own = spread(lax.ppermute(top_hidden, BOTH, TO_READER), BOTH, READERS)
    top_other = lax.ppermute(top_own, "tp", OTHER_CORE)
    total = add_top(True, total, top_own, weight, me, lies)
    total = add_top(False, total, top_other, weight, me, lies)
    merged_parts = lax.all_to_all(total, "dp", 0, 0, tiled=True)
    merged = jnp.sum(merged_parts.astype(jnp.float32), axis=0)

    step = lax.broadcasted_iota(jnp.int32, (tokens, 1), 0) % STEPS
    keep = (step + 1 < jnp.repeat(accepted, STEPS)[:, None]).astype(jnp.float32)
    following = jnp.concatenate([top_hidden[1:], jnp.zeros_like(top_hidden[:1])], axis=0)
    following = jnp.where(step < STEPS - 1, following, jnp.zeros_like(following))
    scale = (CHIPS * tokens) ** (-0.5)
    errors = (keep * (merged - following.astype(jnp.float32)) * scale).astype(jnp.bfloat16)
    errors = spread(errors, "dp")

    tops = [part.reshape(CHIPS * tokens, width) for part in (top_own, top_other)]
    merge_grad = grad(errors, pieces, *tops, me, held)
    return (top_hidden, merge_grad)


def solution(mesh):
    in_specs = (
        P("dp", "tp"),
        P("dp", "tp", None, None),
        P("dp", "tp", None, None),
        P("dp"),
        P("dp"),
        P("dp", "tp"),
        P("dp", "tp"),
        P("dp", "tp"),
        P("tp", None),
        P(None, "dp", "tp"),
    )
    out_specs = (P("dp", "tp"), P(None, "dp", "tp"))
    return jax.shard_map(local, mesh=mesh, in_specs=in_specs, out_specs=out_specs, check_vma=False)
```

```python
import functools

import jax
import jax.numpy as jnp
from jax import lax
from jax.experimental import pallas as pl
from jax.experimental.pallas import tpu as pltpu
from jax.sharding import PartitionSpec as P

STEPS = 4
CHIPS = 8
VMEM = 62 * 2**20


def dev(xl, z, xh, y, c):
    return (xl * 4 + z) * 16 + xh * 8 + y * 2 + c


def coords():
    return [
        (xl, z, xh, y, c)
        for xl in range(2)
        for z in range(4)
        for xh in range(2)
        for y in range(4)
        for c in range(2)
    ]


TO_READER = [(dev(*p), dev(p[2], p[3], p[0], (p[3] - p[1]) % 4, p[4])) for p in coords()]
TO_ACROSS = [(dev(*p), dev(p[2], p[3], 1 - p[0], (p[3] - p[1]) % 4, p[4])) for p in coords()]
READERS = [
    [dev(xl, z, xh, (z - k) % 4, c) for xh in range(2) for k in range(4)]
    for xl in range(2)
    for z in range(4)
    for c in range(2)
]
SAME_CORE = [[2 * t + c for t in range(CHIPS)] for c in range(2)]
OTHER_CORE = [(j, j ^ 1) for j in range(16)]
BOTH = ("dp", "tp")
SCALARS = pl.BlockSpec(memory_space=pltpu.SMEM)
HERE = pl.BlockSpec(memory_space=pltpu.VMEM)
THERE = pl.BlockSpec(memory_space=pl.ANY)
FREE = pl.CostEstimate(flops=0, bytes_accessed=0, transcendentals=0)


def from_y(far):
    return [(j, (j & 8) | (j - 2 * far) % 8) for j in range(16)]


def dot(a, b):
    return jnp.dot(a, b, preferred_element_type=jnp.float32)


def spread(block, axis, groups=None):
    copies = jnp.broadcast_to(block[None], (CHIPS, *block.shape))
    return lax.all_to_all(copies, axis, 0, 0, tiled=True, axis_index_groups=groups)


def fetch(pairs, sems):
    copies = [
        pltpu.make_async_copy(source, target, sems.at[i])
        for i, (source, target) in enumerate(pairs)
    ]
    for copy in copies:
        copy.start()
    return copies


def attend_kernel(lens, queries, keys, values, out, held, scores, weights, gathered, sems):
    rows, width = held.shape[1], keys.shape[2]
    heads = queries.shape[1] // width
    size = heads * STEPS
    copies = fetch(
        [
            (source.at[pl.ds(i * rows // 2, rows // 2)], held.at[j, pl.ds(i * rows // 2, rows // 2)])
            for i in range(2)
            for j, source in enumerate((keys, values))
        ],
        sems,
    )
    shape = (size, keys.shape[1])
    position = lax.broadcasted_iota(jnp.int32, shape, 1)
    step = lax.broadcasted_iota(jnp.int32, shape, 0) % STEPS
    scale = width ** (-0.5)
    for h in range(heads):
        asked = queries[:, h * width : (h + 1) * width].astype(jnp.float32)
        for r in range(rows):
            gathered[r, h * STEPS : (h + 1) * STEPS, :] = asked[r * STEPS : (r + 1) * STEPS]
    for i in range(2):
        copies[2 * i].wait()
        for r in range(i * rows // 2, (i + 1) * rows // 2):
            score = lax.dot_general(
                gathered[r].astype(queries.dtype), held[0, r], (((1,), (1,)), ((), ())), preferred_element_type=jnp.float32
            )
            visible = position < lens[r] + step + 1
            scores[r * size : (r + 1) * size, :] = jnp.where(visible, score * scale, -1e30)
        part = slice(i * rows * size // 2, (i + 1) * rows * size // 2)
        score = scores[part, :]
        expo = jnp.exp(score - jnp.max(score, axis=-1, keepdims=True))
        inverse = 1.0 / jnp.sum(expo, axis=-1, keepdims=True)
        weights[part, :] = (expo * inverse).astype(weights.dtype)
        copies[2 * i + 1].wait()
        for r in range(i * rows // 2, (i + 1) * rows // 2):
            gathered[r] = dot(weights[r * size : (r + 1) * size, :], held[1, r])
    for h in range(heads):
        context = [gathered[r, h * STEPS : (h + 1) * STEPS, :] for r in range(rows)]
        out[:, h * width : (h + 1) * width] = jnp.concatenate(context, axis=0).astype(out.dtype)


def attend(queries, keys, values, lens):
    rows, positions, width = keys.shape
    tokens, depth = queries.shape
    size = STEPS * depth // width
    return pl.pallas_call(
        attend_kernel,
        in_specs=[SCALARS, HERE, THERE, THERE],
        out_specs=HERE,
        out_shape=jax.ShapeDtypeStruct(queries.shape, queries.dtype),
        scratch_shapes=[
            pltpu.VMEM((2, rows, positions, width), jnp.bfloat16),
            pltpu.VMEM((rows * size, positions), jnp.float32),
            pltpu.VMEM((rows * size, positions), jnp.bfloat16),
            pltpu.VMEM((rows, size, width), jnp.float32),
            pltpu.SemaphoreType.DMA((4,)),
        ],
        compiler_params=pltpu.CompilerParams(vmem_limit_bytes=VMEM),
        cost_estimate=FREE,
        name="attend",
    )(lens, queries, keys, values)


def pack_kernel(cuts, *refs):
    *sources, out, held, in_sems, out_sem = refs
    for copy in fetch([(s, held.at[cut]) for s, cut in zip(sources, cuts)], in_sems):
        copy.wait()
    for copy in fetch([(held, out)], out_sem):
        copy.wait()


def pack(arrays, axis):
    shape = list(arrays[0].shape)
    size = shape[axis]
    cuts = [(slice(None),) * axis + (slice(i * size, (i + 1) * size),) for i in range(len(arrays))]
    shape[axis] *= len(arrays)
    return pl.pallas_call(
        functools.partial(pack_kernel, cuts),
        in_specs=[THERE] * len(arrays),
        out_specs=THERE,
        out_shape=jax.ShapeDtypeStruct(shape, arrays[0].dtype),
        scratch_shapes=[
            pltpu.VMEM(shape, arrays[0].dtype),
            pltpu.SemaphoreType.DMA((len(arrays),)),
            pltpu.SemaphoreType.DMA((1,)),
        ],
        compiler_params=pltpu.CompilerParams(vmem_limit_bytes=VMEM),
        cost_estimate=FREE,
        name="pack",
    )(*arrays)


def project_kernel(half, context, weight, out, held, sems):
    width = out.shape[-1]
    copies = fetch(
        [
            (weight.at[:, pl.ds((2 * t + half[0]) * width, width)], held.at[t])
            for t in range(CHIPS)
        ],
        sems,
    )
    for t in range(CHIPS):
        copies[t].wait()
        out[t] = dot(context[...], held[t]).astype(out.dtype)


def project(context, weight, half):
    tokens, depth = context.shape
    width = weight.shape[1] // (2 * CHIPS)
    return pl.pallas_call(
        project_kernel,
        in_specs=[SCALARS, HERE, THERE],
        out_specs=HERE,
        out_shape=jax.ShapeDtypeStruct((CHIPS, tokens, width), jnp.bfloat16),
        scratch_shapes=[
            pltpu.VMEM((CHIPS, depth, width), jnp.bfloat16),
            pltpu.SemaphoreType.DMA((CHIPS,)),
        ],
        compiler_params=pltpu.CompilerParams(vmem_limit_bytes=VMEM),
        cost_estimate=FREE,
        name="project",
    )(half, context, weight)


def base_kernel(core, *refs):
    count = len(refs) - 5
    sources, (weight, out, held, held_weight, sems) = refs[:count], refs[count:]
    copies = fetch(
        [(weight.at[k], held_weight.at[k]) for k in range(2)]
        + [(source, held.at[i]) for i, source in enumerate(sources)],
        sems,
    )
    half = core[0]
    width = out.shape[-1]
    rows = sources[0].shape[0]
    copies[0].wait()
    copies[1].wait()
    for i in range(count // 2):
        copies[2 + 2 * i].wait()
        copies[3 + 2 * i].wait()
        total = dot(held[2 * i, :, :width], held_weight[0, half])
        total += dot(held[2 * i, :, width:], held_weight[1, half])
        total += dot(held[2 * i + 1, :, :width], held_weight[0, 1 - half])
        total += dot(held[2 * i + 1, :, width:], held_weight[1, 1 - half])
        out[i * rows : (i + 1) * rows, :] = total.astype(out.dtype)


def base(pieces, weight, core):
    rows, depth = pieces[0].shape
    tokens, width = len(pieces) // 2 * rows, depth // 2
    return pl.pallas_call(
        base_kernel,
        in_specs=[SCALARS] + [THERE] * (len(pieces) + 1),
        out_specs=HERE,
        out_shape=jax.ShapeDtypeStruct((tokens, width), jnp.bfloat16),
        scratch_shapes=[
            pltpu.VMEM((len(pieces), rows, depth), jnp.bfloat16),
            pltpu.VMEM((2, *weight.shape[1:]), jnp.bfloat16),
            pltpu.SemaphoreType.DMA((len(pieces) + 2,)),
        ],
        compiler_params=pltpu.CompilerParams(vmem_limit_bytes=VMEM),
        cost_estimate=FREE,
        name="base",
    )(core, *pieces, weight)


def add_kernel(own, core, places, *refs):
    *totals, source, weight, out, held, near, held_weight, sems = refs
    blocks, rows, width = source.shape
    half = core[0] if own else 1 - core[0]
    pairs = [(weight.at[2, half], held_weight)]
    if own:
        order = (0, 1, 2, 3, 6, 7, 4, 5)
        lies = [(total, i) for total in totals for i in range(total.shape[0] // rows)]
        pairs += [
            (total.at[pl.ds(i * rows, rows)], held.at[places[b]])
            for (total, i), b in zip(lies, order)
        ]
        pairs += [(source, near)]
    else:
        for p in range(0, blocks, 2):
            pairs.append((source.at[p : p + 2], near.at[p : p + 2]))
            pairs.append((totals[0].at[p : p + 2], held.at[p : p + 2]))
    copies = fetch(pairs, sems.at[pl.ds(0, len(pairs))])
    copies[0].wait()
    if own:
        for copy in copies[1:]:
            copy.wait()
    for p in range(0, blocks, 2):
        if not own:
            copies[1 + p].wait()
            copies[2 + p].wait()
        added = dot(near[p : p + 2].reshape(2 * rows, width), held_weight[...])
        added = added.reshape(2, rows, width) + held[p : p + 2].astype(jnp.float32)
        out[p : p + 2] = added.astype(out.dtype)


def add_top(own, totals, source, weight, core, places):
    return pl.pallas_call(
        functools.partial(add_kernel, own),
        in_specs=[SCALARS] * 2 + [THERE] * (2 + len(totals)),
        out_specs=HERE,
        out_shape=jax.ShapeDtypeStruct(source.shape, source.dtype),
        scratch_shapes=[
            pltpu.VMEM(source.shape, source.dtype),
            pltpu.VMEM(source.shape, source.dtype),
            pltpu.VMEM(weight.shape[2:], weight.dtype),
            pltpu.SemaphoreType.DMA((10,)),
        ],
        compiler_params=pltpu.CompilerParams(vmem_limit_bytes=VMEM),
        cost_estimate=FREE,
        name="add_top",
    )(core, places, *totals, source, weight)


def grad_kernel(core, places, errors, *refs):
    count = len(refs) - 10
    boths, refs = refs[:count], refs[count:]
    top_own, top_other, out, near, ordered, held, tops, made, sems, out_sems = refs
    blocks, rows, width = errors.shape
    tokens = blocks * rows
    pairs = [(errors, near)]
    pairs += [(boths[i], held.at[0, i // 2]) for i in range(0, count, 2)]
    first = fetch(pairs, sems.at[pl.ds(0, len(pairs))])
    rest = [(boths[i], held.at[1, i // 2]) for i in range(1, count, 2)]
    rest += [(top_own, tops.at[0]), (top_other, tops.at[1])]
    first[0].wait()
    for p in range(blocks):
        ordered[p * rows : (p + 1) * rows, :] = near[places[p]]
    for copy in first[1:]:
        copy.wait()
    rest = fetch(rest, sems.at[pl.ds(len(pairs), len(rest))])
    sent = []
    for i in range(6):
        if i == 2:
            for copy in rest[: count // 2]:
                copy.wait()
        if i >= 4:
            rest[count // 2 + i - 4].wait()
        half = 1 - core[0] if i in (2, 3, 5) else core[0]
        for part in range(2):
            step, cut = 2 * i + part, width // 2
            slot = step % made.shape[0]
            if step >= made.shape[0]:
                sent[step - made.shape[0]].wait()
            if i < 4:
                begin = i % 2 * width + part * cut
                source = held[i // 2, :, :, begin : begin + cut].reshape(tokens, cut)
                against = ordered[...]
            else:
                source = tops[i - 4, :, part * cut : (part + 1) * cut]
                against = near[...].reshape(tokens, width)
            made[slot] = lax.dot_general(
                source, against, (((0,), (0,)), ((), ())), preferred_element_type=jnp.float32
            )
            target = out.at[i % 2 if i < 4 else 2, pl.ds(half * width + part * cut, cut)]
            copy = pltpu.make_async_copy(made.at[slot], target, out_sems.at[step])
            copy.start()
            sent.append(copy)
    for copy in sent[-made.shape[0] :]:
        copy.wait()


def grad(errors, boths, tops, core, places):
    blocks, rows, width = errors.shape
    tokens = blocks * rows
    count = len(boths)
    return pl.pallas_call(
        grad_kernel,
        in_specs=[SCALARS] * 2 + [THERE] * (count + 3),
        out_specs=THERE,
        out_shape=jax.ShapeDtypeStruct((3, 2 * width, width), jnp.float32),
        scratch_shapes=[
            pltpu.VMEM(errors.shape, jnp.bfloat16),
            pltpu.VMEM((tokens, width), jnp.bfloat16),
            pltpu.VMEM((2, count // 2, *boths[0].shape), jnp.bfloat16),
            pltpu.VMEM((2, tokens, width), jnp.bfloat16),
            pltpu.VMEM((4, width // 2, width), jnp.float32),
            pltpu.SemaphoreType.DMA((count + 3,)),
            pltpu.SemaphoreType.DMA((12,)),
        ],
        compiler_params=pltpu.CompilerParams(vmem_limit_bytes=VMEM),
        cost_estimate=FREE,
        name="grad",
    )(core, places, errors, *boths, *tops)


def local(
    queries,
    keys_cache,
    values_cache,
    prefix_len,
    accepted,
    residual_in,
    low_hidden,
    mid_hidden,
    out_weight,
    merge_weight,
):
    tokens, width = residual_in.shape
    me_dp, me_tp = lax.axis_index("dp"), lax.axis_index("tp")
    xl, z = me_dp // 4, me_dp % 4
    xh, y, core = me_tp // 8, me_tp // 2 % 4, me_tp % 2
    me = core.reshape(1)
    index = jnp.arange(CHIPS)
    held = ((xh ^ (index % 2)) * 4 + (z - y - index // 2) % 4).astype(jnp.int32)
    weight = merge_weight.reshape(3, 2, width, width)

    both = pack([low_hidden, mid_hidden], 1)
    both = [lax.ppermute(both, BOTH, way) for way in (TO_READER, TO_ACROSS)]
    context = attend(queries, keys_cache[:, 0], values_cache[:, 0], prefix_len)
    taken = project(context, out_weight, 1 - me)
    taken, *both = lax.optimization_barrier((taken, *both))
    both = pack(both, 0)
    both = [both] + [lax.ppermute(both, "tp", from_y(far)) for far in (1, 2, 3)]
    taken = lax.ppermute(taken, "tp", OTHER_CORE)
    kept = project(context, out_weight, me)
    pair = (kept.astype(jnp.float32) + taken.astype(jnp.float32)).astype(jnp.bfloat16)
    pair, both[1], both[3] = lax.optimization_barrier((pair, both[1], both[3]))
    parts = lax.all_to_all(pair, "tp", 0, 0, tiled=True, axis_index_groups=SAME_CORE)
    summed = jnp.sum(parts.astype(jnp.float32), axis=0)
    top_hidden = (residual_in.astype(jnp.float32) + summed).astype(jnp.bfloat16)

    def twins(pieces):
        return [half for piece in pieces for half in (piece, lax.ppermute(piece, "tp", OTHER_CORE))]

    first = twins([both[0], both[1], both[3]])
    total = base(first, weight, me)
    top_hidden, total, held = lax.optimization_barrier((top_hidden, total, held))

    top_moved = lax.ppermute(top_hidden, BOTH, TO_READER)
    second = twins([both[2]])
    rest = base(second, weight, me)
    top_own = spread(top_moved, BOTH, READERS)
    top_own, rest = lax.optimization_barrier((top_own, rest))
    top_other = lax.ppermute(top_own, "tp", OTHER_CORE)
    total = add_top(True, (total, rest), top_own, weight, me, held)
    total = add_top(False, (total,), top_other, weight, me, held)
    merged_parts = lax.all_to_all(total, "dp", 0, 0, tiled=True)
    merged = jnp.sum(merged_parts.astype(jnp.float32), axis=0)

    step = lax.broadcasted_iota(jnp.int32, (tokens, 1), 0) % STEPS
    keep = (step + 1 < jnp.repeat(accepted, STEPS)[:, None]).astype(jnp.float32)
    following = jnp.concatenate([top_hidden[1:], jnp.zeros_like(top_hidden[:1])], axis=0)
    following = jnp.where(step < STEPS - 1, following, jnp.zeros_like(following))
    scale = (CHIPS * tokens) ** (-0.5)
    errors = (keep * (merged - following.astype(jnp.float32)) * scale).astype(jnp.bfloat16)
    errors = spread(errors, "dp")

    boths = first[:4] + second + first[4:]
    tops = [part.reshape(CHIPS * tokens, width) for part in (top_own, top_other)]
    merge_grad = grad(errors, boths, tops, me, held)
    return (top_hidden, merge_grad)


def solution(mesh):
    in_specs = (
        P("dp", "tp"),
        P("dp", "tp", None, None),
        P("dp", "tp", None, None),
        P("dp"),
        P("dp"),
        P("dp", "tp"),
        P("dp", "tp"),
        P("dp", "tp"),
        P("tp", None),
        P(None, "dp", "tp"),
    )
    out_specs = (P("dp", "tp"), P(None, "dp", "tp"))
    return jax.shard_map(local, mesh=mesh, in_specs=in_specs, out_specs=out_specs, check_vma=False)
```

```python
import functools

import jax
import jax.numpy as jnp
from jax import lax
from jax.experimental import pallas as pl
from jax.experimental.pallas import tpu as pltpu
from jax.sharding import PartitionSpec as P

STEPS = 4
CHIPS = 8
VMEM = 62 * 2**20


def dev(xl, z, xh, y, c):
    return (xl * 4 + z) * 16 + xh * 8 + y * 2 + c


def coords():
    return [
        (xl, z, xh, y, c)
        for xl in range(2)
        for z in range(4)
        for xh in range(2)
        for y in range(4)
        for c in range(2)
    ]


TO_READER = [(dev(*p), dev(p[2], p[3], p[0], (p[3] - p[1]) % 4, p[4])) for p in coords()]
TO_ACROSS = [(dev(*p), dev(p[2], p[3], 1 - p[0], (p[3] - p[1]) % 4, p[4])) for p in coords()]
READERS = [
    [dev(xl, z, xh, (z - k) % 4, c) for xh in range(2) for k in range(4)]
    for xl in range(2)
    for z in range(4)
    for c in range(2)
]
SAME_CORE = [[2 * t + c for t in range(CHIPS)] for c in range(2)]
OTHER_CORE = [(j, j ^ 1) for j in range(16)]
BOTH = ("dp", "tp")
SCALARS = pl.BlockSpec(memory_space=pltpu.SMEM)
HERE = pl.BlockSpec(memory_space=pltpu.VMEM)
THERE = pl.BlockSpec(memory_space=pl.ANY)
FREE = pl.CostEstimate(flops=0, bytes_accessed=0, transcendentals=0)


def from_y(far):
    return [(j, (j & 8) | (j - 2 * far) % 8) for j in range(16)]


def dot(a, b):
    return jnp.dot(a, b, preferred_element_type=jnp.float32)


def spread(block, axis, groups=None):
    copies = jnp.broadcast_to(block[None], (CHIPS, *block.shape))
    return lax.all_to_all(copies, axis, 0, 0, tiled=True, axis_index_groups=groups)


def fetch(pairs, sems):
    copies = [
        pltpu.make_async_copy(source, target, sems.at[i])
        for i, (source, target) in enumerate(pairs)
    ]
    for copy in copies:
        copy.start()
    return copies


def attend_kernel(lens, queries, keys, values, out, held, scores, weights, gathered, sems):
    rows, width = held.shape[1], keys.shape[2]
    heads = queries.shape[1] // width
    size = heads * STEPS
    copies = fetch(
        [
            (source.at[pl.ds(i * rows // 2, rows // 2)], held.at[j, pl.ds(i * rows // 2, rows // 2)])
            for i in range(2)
            for j, source in enumerate((keys, values))
        ],
        sems,
    )
    shape = (size, keys.shape[1])
    position = lax.broadcasted_iota(jnp.int32, shape, 1)
    step = lax.broadcasted_iota(jnp.int32, shape, 0) % STEPS
    scale = width ** (-0.5)
    for h in range(heads):
        asked = queries[:, h * width : (h + 1) * width].astype(jnp.float32)
        for r in range(rows):
            gathered[r, h * STEPS : (h + 1) * STEPS, :] = asked[r * STEPS : (r + 1) * STEPS]
    for i in range(2):
        copies[2 * i].wait()
        for r in range(i * rows // 2, (i + 1) * rows // 2):
            score = lax.dot_general(
                gathered[r].astype(queries.dtype), held[0, r], (((1,), (1,)), ((), ())), preferred_element_type=jnp.float32
            )
            visible = position < lens[r] + step + 1
            scores[r * size : (r + 1) * size, :] = jnp.where(visible, score * scale, -1e30)
        part = slice(i * rows * size // 2, (i + 1) * rows * size // 2)
        score = scores[part, :]
        expo = jnp.exp(score - jnp.max(score, axis=-1, keepdims=True))
        inverse = 1.0 / jnp.sum(expo, axis=-1, keepdims=True)
        weights[part, :] = (expo * inverse).astype(weights.dtype)
        copies[2 * i + 1].wait()
        for r in range(i * rows // 2, (i + 1) * rows // 2):
            gathered[r] = dot(weights[r * size : (r + 1) * size, :], held[1, r])
    for h in range(heads):
        context = [gathered[r, h * STEPS : (h + 1) * STEPS, :] for r in range(rows)]
        out[:, h * width : (h + 1) * width] = jnp.concatenate(context, axis=0).astype(out.dtype)


def attend(queries, keys, values, lens):
    rows, positions, width = keys.shape
    tokens, depth = queries.shape
    size = STEPS * depth // width
    return pl.pallas_call(
        attend_kernel,
        in_specs=[SCALARS, HERE, THERE, THERE],
        out_specs=HERE,
        out_shape=jax.ShapeDtypeStruct(queries.shape, queries.dtype),
        scratch_shapes=[
            pltpu.VMEM((2, rows, positions, width), jnp.bfloat16),
            pltpu.VMEM((rows * size, positions), jnp.float32),
            pltpu.VMEM((rows * size, positions), jnp.bfloat16),
            pltpu.VMEM((rows, size, width), jnp.float32),
            pltpu.SemaphoreType.DMA((4,)),
        ],
        compiler_params=pltpu.CompilerParams(vmem_limit_bytes=VMEM),
        cost_estimate=FREE,
        name="attend",
    )(lens, queries, keys, values)


def pack_kernel(cuts, *refs):
    *sources, out, held, in_sems, out_sem = refs
    for copy in fetch([(s, held.at[cut]) for s, cut in zip(sources, cuts)], in_sems):
        copy.wait()
    for copy in fetch([(held, out)], out_sem):
        copy.wait()


def pack(arrays, axis):
    shape = list(arrays[0].shape)
    size = shape[axis]
    cuts = [(slice(None),) * axis + (slice(i * size, (i + 1) * size),) for i in range(len(arrays))]
    shape[axis] *= len(arrays)
    return pl.pallas_call(
        functools.partial(pack_kernel, cuts),
        in_specs=[THERE] * len(arrays),
        out_specs=THERE,
        out_shape=jax.ShapeDtypeStruct(shape, arrays[0].dtype),
        scratch_shapes=[
            pltpu.VMEM(shape, arrays[0].dtype),
            pltpu.SemaphoreType.DMA((len(arrays),)),
            pltpu.SemaphoreType.DMA((1,)),
        ],
        compiler_params=pltpu.CompilerParams(vmem_limit_bytes=VMEM),
        cost_estimate=FREE,
        name="pack",
    )(*arrays)


def project_kernel(half, context, weight, out, held, sems):
    width = out.shape[-1]
    copies = fetch(
        [
            (weight.at[:, pl.ds((2 * t + half[0]) * width, width)], held.at[t])
            for t in range(CHIPS)
        ],
        sems,
    )
    for t in range(CHIPS):
        copies[t].wait()
        out[t] = dot(context[...], held[t]).astype(out.dtype)


def project(context, weight, half):
    tokens, depth = context.shape
    width = weight.shape[1] // (2 * CHIPS)
    return pl.pallas_call(
        project_kernel,
        in_specs=[SCALARS, HERE, THERE],
        out_specs=HERE,
        out_shape=jax.ShapeDtypeStruct((CHIPS, tokens, width), jnp.bfloat16),
        scratch_shapes=[
            pltpu.VMEM((CHIPS, depth, width), jnp.bfloat16),
            pltpu.SemaphoreType.DMA((CHIPS,)),
        ],
        compiler_params=pltpu.CompilerParams(vmem_limit_bytes=VMEM),
        cost_estimate=FREE,
        name="project",
    )(half, context, weight)


def base_kernel(core, *refs):
    count = len(refs) - 5
    sources, (weight, out, held, held_weight, sems) = refs[:count], refs[count:]
    copies = fetch(
        [(weight.at[k], held_weight.at[k]) for k in range(2)]
        + [(source, held.at[i]) for i, source in enumerate(sources)],
        sems,
    )
    half = core[0]
    width = out.shape[-1]
    rows = sources[0].shape[0]
    copies[0].wait()
    copies[1].wait()
    for i in range(count // 2):
        copies[2 + 2 * i].wait()
        copies[3 + 2 * i].wait()
        total = dot(held[2 * i, :, :width], held_weight[0, half])
        total += dot(held[2 * i, :, width:], held_weight[1, half])
        total += dot(held[2 * i + 1, :, :width], held_weight[0, 1 - half])
        total += dot(held[2 * i + 1, :, width:], held_weight[1, 1 - half])
        out[i * rows : (i + 1) * rows, :] = total.astype(out.dtype)


def base(pieces, weight, core):
    rows, depth = pieces[0].shape
    tokens, width = len(pieces) // 2 * rows, depth // 2
    return pl.pallas_call(
        base_kernel,
        in_specs=[SCALARS] + [THERE] * (len(pieces) + 1),
        out_specs=HERE,
        out_shape=jax.ShapeDtypeStruct((tokens, width), jnp.bfloat16),
        scratch_shapes=[
            pltpu.VMEM((len(pieces), rows, depth), jnp.bfloat16),
            pltpu.VMEM((2, *weight.shape[1:]), jnp.bfloat16),
            pltpu.SemaphoreType.DMA((len(pieces) + 2,)),
        ],
        compiler_params=pltpu.CompilerParams(vmem_limit_bytes=VMEM),
        cost_estimate=FREE,
        name="base",
    )(core, *pieces, weight)


def join_kernel(core, places, total, rest, own, other, weight, out, held, near, held_weight, made, sems, out_sems):
    blocks, rows, width = own.shape
    order = (0, 1, 2, 3, 6, 7, 4, 5)
    lies = [(part, i) for part in (total, rest) for i in range(part.shape[0] // rows)]
    pairs = [(weight.at[2], held_weight)]
    pairs += [
        (part.at[pl.ds(i * rows, rows)], held.at[places[b]]) for (part, i), b in zip(lies, order)
    ]
    for p in range(0, blocks, 2):
        pairs += [(part.at[p : p + 2], near.at[i, p : p + 2]) for i, part in enumerate((own, other))]
    copies = fetch(pairs, sems)
    for copy in copies[: 1 + blocks]:
        copy.wait()
    sent = []
    for p in range(0, blocks, 2):
        copies[1 + blocks + p].wait()
        copies[2 + blocks + p].wait()
        joined = dot(near[0, p : p + 2].reshape(2 * rows, width), held_weight[core[0]])
        joined += dot(near[1, p : p + 2].reshape(2 * rows, width), held_weight[1 - core[0]])
        joined = joined.reshape(2, rows, width) + held[p : p + 2].astype(jnp.float32)
        made[p : p + 2] = joined.astype(made.dtype)
        sent += fetch([(made.at[p : p + 2], out.at[p : p + 2])], out_sems.at[pl.ds(p // 2, 1)])
    for copy in sent:
        copy.wait()


def join(total, rest, own, other, weight, core, places):
    blocks, rows, width = own.shape
    return pl.pallas_call(
        join_kernel,
        in_specs=[SCALARS] * 2 + [THERE] * 5,
        out_specs=THERE,
        out_shape=jax.ShapeDtypeStruct(own.shape, own.dtype),
        scratch_shapes=[
            pltpu.VMEM(own.shape, own.dtype),
            pltpu.VMEM((2, *own.shape), own.dtype),
            pltpu.VMEM(weight.shape[1:], weight.dtype),
            pltpu.VMEM(own.shape, own.dtype),
            pltpu.SemaphoreType.DMA((1 + 2 * blocks,)),
            pltpu.SemaphoreType.DMA((blocks // 2,)),
        ],
        compiler_params=pltpu.CompilerParams(vmem_limit_bytes=VMEM),
        cost_estimate=FREE,
        name="join",
    )(core, places, total, rest, own, other, weight)


def grad_kernel(core, places, errors, *refs):
    count = len(refs) - 10
    boths, refs = refs[:count], refs[count:]
    top_own, top_other, out, near, ordered, held, tops, made, sems, out_sems = refs
    blocks, rows, width = errors.shape
    tokens = blocks * rows
    pairs = [(errors, near)]
    pairs += [(boths[i], held.at[0, i // 2]) for i in range(0, count, 2)]
    first = fetch(pairs, sems.at[pl.ds(0, len(pairs))])
    rest = [(boths[i], held.at[1, i // 2]) for i in range(1, count, 2)]
    rest += [(top_own, tops.at[0]), (top_other, tops.at[1])]
    first[0].wait()
    rest = fetch(rest, sems.at[pl.ds(len(pairs), len(rest))])
    for p in range(blocks):
        ordered[p * rows : (p + 1) * rows, :] = near[places[p]]
    for copy in first[1:]:
        copy.wait()
    sent = []
    for i in range(6):
        if i == 2:
            for copy in rest[: count // 2]:
                copy.wait()
        if i >= 4:
            rest[count // 2 + i - 4].wait()
        half = 1 - core[0] if i in (2, 3, 5) else core[0]
        for part in range(2):
            step, cut = 2 * i + part, width // 2
            slot = step % made.shape[0]
            if step >= made.shape[0]:
                sent[step - made.shape[0]].wait()
            if i < 4:
                begin = i % 2 * width + part * cut
                source = held[i // 2, :, :, begin : begin + cut].reshape(tokens, cut)
                against = ordered[...]
            else:
                source = tops[i - 4, :, part * cut : (part + 1) * cut]
                against = near[...].reshape(tokens, width)
            made[slot] = lax.dot_general(
                source, against, (((0,), (0,)), ((), ())), preferred_element_type=jnp.float32
            )
            target = out.at[i % 2 if i < 4 else 2, pl.ds(half * width + part * cut, cut)]
            copy = pltpu.make_async_copy(made.at[slot], target, out_sems.at[step])
            copy.start()
            sent.append(copy)
    for copy in sent[-made.shape[0] :]:
        copy.wait()


def grad(errors, boths, tops, core, places):
    blocks, rows, width = errors.shape
    tokens = blocks * rows
    count = len(boths)
    return pl.pallas_call(
        grad_kernel,
        in_specs=[SCALARS] * 2 + [THERE] * (count + 3),
        out_specs=THERE,
        out_shape=jax.ShapeDtypeStruct((3, 2 * width, width), jnp.float32),
        scratch_shapes=[
            pltpu.VMEM(errors.shape, jnp.bfloat16),
            pltpu.VMEM((tokens, width), jnp.bfloat16),
            pltpu.VMEM((2, count // 2, *boths[0].shape), jnp.bfloat16),
            pltpu.VMEM((2, tokens, width), jnp.bfloat16),
            pltpu.VMEM((4, width // 2, width), jnp.float32),
            pltpu.SemaphoreType.DMA((count + 3,)),
            pltpu.SemaphoreType.DMA((12,)),
        ],
        compiler_params=pltpu.CompilerParams(vmem_limit_bytes=VMEM),
        cost_estimate=FREE,
        name="grad",
    )(core, places, errors, *boths, *tops)


def local(
    queries,
    keys_cache,
    values_cache,
    prefix_len,
    accepted,
    residual_in,
    low_hidden,
    mid_hidden,
    out_weight,
    merge_weight,
):
    tokens, width = residual_in.shape
    me_dp, me_tp = lax.axis_index("dp"), lax.axis_index("tp")
    xl, z = me_dp // 4, me_dp % 4
    xh, y, core = me_tp // 8, me_tp // 2 % 4, me_tp % 2
    me = core.reshape(1)
    index = jnp.arange(CHIPS)
    held = ((xh ^ (index % 2)) * 4 + (z - y - index // 2) % 4).astype(jnp.int32)
    weight = merge_weight.reshape(3, 2, width, width)

    both = pack([low_hidden, mid_hidden], 1)
    both = [lax.ppermute(both, BOTH, way) for way in (TO_READER, TO_ACROSS)]
    context = attend(queries, keys_cache[:, 0], values_cache[:, 0], prefix_len)
    taken = project(context, out_weight, 1 - me)
    taken, *both = lax.optimization_barrier((taken, *both))
    both = pack(both, 0)
    both = [both] + [lax.ppermute(both, "tp", from_y(far)) for far in (1, 2, 3)]
    taken = lax.ppermute(taken, "tp", OTHER_CORE)
    kept = project(context, out_weight, me)
    pair = (kept.astype(jnp.float32) + taken.astype(jnp.float32)).astype(jnp.bfloat16)
    pair, both[1], both[3] = lax.optimization_barrier((pair, both[1], both[3]))
    parts = lax.all_to_all(pair, "tp", 0, 0, tiled=True, axis_index_groups=SAME_CORE)
    summed = jnp.sum(parts.astype(jnp.float32), axis=0)
    top_hidden = (residual_in.astype(jnp.float32) + summed).astype(jnp.bfloat16)

    def twins(pieces):
        return [half for piece in pieces for half in (piece, lax.ppermute(piece, "tp", OTHER_CORE))]

    first = twins([both[0], both[1], both[3]])
    total = base(first, weight, me)
    top_hidden, total, held = lax.optimization_barrier((top_hidden, total, held))

    top_moved = lax.ppermute(top_hidden, BOTH, TO_READER)
    second = twins([both[2]])
    rest = base(second, weight, me)
    top_own = spread(top_moved, BOTH, READERS)
    top_own, rest = lax.optimization_barrier((top_own, rest))
    top_other = lax.ppermute(top_own, "tp", OTHER_CORE)
    total = join(total, rest, top_own, top_other, weight, me, held)
    merged_parts = lax.all_to_all(total, "dp", 0, 0, tiled=True)
    merged = jnp.sum(merged_parts.astype(jnp.float32), axis=0)

    step = lax.broadcasted_iota(jnp.int32, (tokens, 1), 0) % STEPS
    keep = (step + 1 < jnp.repeat(accepted, STEPS)[:, None]).astype(jnp.float32)
    following = jnp.concatenate([top_hidden[1:], jnp.zeros_like(top_hidden[:1])], axis=0)
    following = jnp.where(step < STEPS - 1, following, jnp.zeros_like(following))
    scale = (CHIPS * tokens) ** (-0.5)
    errors = (keep * (merged - following.astype(jnp.float32)) * scale).astype(jnp.bfloat16)
    errors = spread(errors, "dp")

    boths = first[:4] + second + first[4:]
    tops = [part.reshape(CHIPS * tokens, width) for part in (top_own, top_other)]
    merge_grad = grad(errors, boths, tops, me, held)
    return (top_hidden, merge_grad)


def solution(mesh):
    in_specs = (
        P("dp", "tp"),
        P("dp", "tp", None, None),
        P("dp", "tp", None, None),
        P("dp"),
        P("dp"),
        P("dp", "tp"),
        P("dp", "tp"),
        P("dp", "tp"),
        P("tp", None),
        P(None, "dp", "tp"),
    )
    out_specs = (P("dp", "tp"), P(None, "dp", "tp"))
    return jax.shard_map(local, mesh=mesh, in_specs=in_specs, out_specs=out_specs, check_vma=False)
```

```python
import functools

import jax
import jax.numpy as jnp
from jax import lax
from jax.experimental import pallas as pl
from jax.experimental.pallas import tpu as pltpu
from jax.sharding import PartitionSpec as P

STEPS = 4
CHIPS = 8
VMEM = 62 * 2**20


def dev(xl, z, xh, y, c):
    return (xl * 4 + z) * 16 + xh * 8 + y * 2 + c


def coords():
    return [
        (xl, z, xh, y, c)
        for xl in range(2)
        for z in range(4)
        for xh in range(2)
        for y in range(4)
        for c in range(2)
    ]


TO_READER = [(dev(*p), dev(p[2], p[3], p[0], (p[3] - p[1]) % 4, p[4])) for p in coords()]
TO_ACROSS = [(dev(*p), dev(p[2], p[3], 1 - p[0], (p[3] - p[1]) % 4, p[4])) for p in coords()]
READERS = [
    [dev(xl, z, xh, (z - k) % 4, c) for xh in range(2) for k in range(4)]
    for xl in range(2)
    for z in range(4)
    for c in range(2)
]
SAME_CORE = [[2 * t + c for t in range(CHIPS)] for c in range(2)]
OTHER_CORE = [(j, j ^ 1) for j in range(16)]
BOTH = ("dp", "tp")
SCALARS = pl.BlockSpec(memory_space=pltpu.SMEM)
HERE = pl.BlockSpec(memory_space=pltpu.VMEM)
THERE = pl.BlockSpec(memory_space=pl.ANY)
FREE = pl.CostEstimate(flops=0, bytes_accessed=0, transcendentals=0)


def from_y(far):
    return [(j, (j & 8) | (j - 2 * far) % 8) for j in range(16)]


def dot(a, b):
    return jnp.dot(a, b, preferred_element_type=jnp.float32)


def spread(block, axis, groups=None):
    copies = jnp.broadcast_to(block[None], (CHIPS, *block.shape))
    return lax.all_to_all(copies, axis, 0, 0, tiled=True, axis_index_groups=groups)


def fetch(pairs, sems):
    copies = [
        pltpu.make_async_copy(source, target, sems.at[i])
        for i, (source, target) in enumerate(pairs)
    ]
    for copy in copies:
        copy.start()
    return copies


def attend_kernel(lens, half, queries, keys, values, weight, out, made, held, scores, weights, gathered, strips, sems, strip_sems):
    rows, width = held.shape[1], keys.shape[2]
    heads = queries.shape[1] // width
    size = heads * STEPS
    copies = fetch(
        [
            (source.at[pl.ds(i * rows // 2, rows // 2)], held.at[j, pl.ds(i * rows // 2, rows // 2)])
            for i in range(2)
            for j, source in enumerate((keys, values))
        ],
        sems,
    )
    cut = made.shape[-1]
    arriving = fetch(
        [
            (weight.at[:, pl.ds((2 * t + half[0]) * cut, cut)], strips.at[t])
            for t in range(CHIPS)
        ],
        strip_sems,
    )
    shape = (size, keys.shape[1])
    position = lax.broadcasted_iota(jnp.int32, shape, 1)
    step = lax.broadcasted_iota(jnp.int32, shape, 0) % STEPS
    scale = width ** (-0.5)
    for h in range(heads):
        asked = queries[:, h * width : (h + 1) * width].astype(jnp.float32)
        for r in range(rows):
            gathered[r, h * STEPS : (h + 1) * STEPS, :] = asked[r * STEPS : (r + 1) * STEPS]
    for i in range(2):
        copies[2 * i].wait()
        for r in range(i * rows // 2, (i + 1) * rows // 2):
            score = lax.dot_general(
                gathered[r].astype(queries.dtype), held[0, r], (((1,), (1,)), ((), ())), preferred_element_type=jnp.float32
            )
            visible = position < lens[r] + step + 1
            scores[r * size : (r + 1) * size, :] = jnp.where(visible, score * scale, -1e30)
        part = slice(i * rows * size // 2, (i + 1) * rows * size // 2)
        score = scores[part, :]
        expo = jnp.exp(score - jnp.max(score, axis=-1, keepdims=True))
        inverse = 1.0 / jnp.sum(expo, axis=-1, keepdims=True)
        weights[part, :] = (expo * inverse).astype(weights.dtype)
        copies[2 * i + 1].wait()
        for r in range(i * rows // 2, (i + 1) * rows // 2):
            gathered[r] = dot(weights[r * size : (r + 1) * size, :], held[1, r])
    for h in range(heads):
        context = [gathered[r, h * STEPS : (h + 1) * STEPS, :] for r in range(rows)]
        out[:, h * width : (h + 1) * width] = jnp.concatenate(context, axis=0).astype(out.dtype)
    for t in range(CHIPS):
        arriving[t].wait()
        made[t] = dot(out[...], strips[t]).astype(made.dtype)


def attend(queries, keys, values, lens, weight, half):
    rows, positions, width = keys.shape
    tokens, depth = queries.shape
    size = STEPS * depth // width
    cut = weight.shape[1] // (2 * CHIPS)
    return pl.pallas_call(
        attend_kernel,
        in_specs=[SCALARS, SCALARS, HERE, THERE, THERE, THERE],
        out_specs=[HERE, HERE],
        out_shape=[
            jax.ShapeDtypeStruct(queries.shape, queries.dtype),
            jax.ShapeDtypeStruct((CHIPS, tokens, cut), jnp.bfloat16),
        ],
        scratch_shapes=[
            pltpu.VMEM((2, rows, positions, width), jnp.bfloat16),
            pltpu.VMEM((rows * size, positions), jnp.float32),
            pltpu.VMEM((rows * size, positions), jnp.bfloat16),
            pltpu.VMEM((rows, size, width), jnp.float32),
            pltpu.VMEM((CHIPS, depth, cut), jnp.bfloat16),
            pltpu.SemaphoreType.DMA((4,)),
            pltpu.SemaphoreType.DMA((CHIPS,)),
        ],
        compiler_params=pltpu.CompilerParams(vmem_limit_bytes=VMEM),
        cost_estimate=FREE,
        name="attend",
    )(lens, half, queries, keys, values, weight)


def pack_kernel(cuts, *refs):
    *sources, out, held, in_sems, out_sem = refs
    for copy in fetch([(s, held.at[cut]) for s, cut in zip(sources, cuts)], in_sems):
        copy.wait()
    for copy in fetch([(held, out)], out_sem):
        copy.wait()


def pack(arrays, axis):
    shape = list(arrays[0].shape)
    size = shape[axis]
    cuts = [(slice(None),) * axis + (slice(i * size, (i + 1) * size),) for i in range(len(arrays))]
    shape[axis] *= len(arrays)
    return pl.pallas_call(
        functools.partial(pack_kernel, cuts),
        in_specs=[THERE] * len(arrays),
        out_specs=THERE,
        out_shape=jax.ShapeDtypeStruct(shape, arrays[0].dtype),
        scratch_shapes=[
            pltpu.VMEM(shape, arrays[0].dtype),
            pltpu.SemaphoreType.DMA((len(arrays),)),
            pltpu.SemaphoreType.DMA((1,)),
        ],
        compiler_params=pltpu.CompilerParams(vmem_limit_bytes=VMEM),
        cost_estimate=FREE,
        name="pack",
    )(*arrays)


def project_kernel(half, context, weight, out, held, sems):
    width = out.shape[-1]
    copies = fetch(
        [
            (weight.at[:, pl.ds((2 * t + half[0]) * width, width)], held.at[t])
            for t in range(CHIPS)
        ],
        sems,
    )
    for t in range(CHIPS):
        copies[t].wait()
        out[t] = dot(context[...], held[t]).astype(out.dtype)


def project(context, weight, half):
    tokens, depth = context.shape
    width = weight.shape[1] // (2 * CHIPS)
    return pl.pallas_call(
        project_kernel,
        in_specs=[SCALARS, HERE, THERE],
        out_specs=HERE,
        out_shape=jax.ShapeDtypeStruct((CHIPS, tokens, width), jnp.bfloat16),
        scratch_shapes=[
            pltpu.VMEM((CHIPS, depth, width), jnp.bfloat16),
            pltpu.SemaphoreType.DMA((CHIPS,)),
        ],
        compiler_params=pltpu.CompilerParams(vmem_limit_bytes=VMEM),
        cost_estimate=FREE,
        name="project",
    )(half, context, weight)


def base_kernel(core, *refs):
    count = len(refs) - 5
    sources, (weight, out, held, held_weight, sems) = refs[:count], refs[count:]
    copies = fetch(
        [(weight.at[k], held_weight.at[k]) for k in range(2)]
        + [(source, held.at[i]) for i, source in enumerate(sources)],
        sems,
    )
    half = core[0]
    width = out.shape[-1]
    rows = sources[0].shape[0]
    copies[0].wait()
    copies[1].wait()
    for i in range(count // 2):
        copies[2 + 2 * i].wait()
        copies[3 + 2 * i].wait()
        total = dot(held[2 * i, :, :width], held_weight[0, half])
        total += dot(held[2 * i, :, width:], held_weight[1, half])
        total += dot(held[2 * i + 1, :, :width], held_weight[0, 1 - half])
        total += dot(held[2 * i + 1, :, width:], held_weight[1, 1 - half])
        out[i * rows : (i + 1) * rows, :] = total.astype(out.dtype)


def base(pieces, weight, core):
    rows, depth = pieces[0].shape
    tokens, width = len(pieces) // 2 * rows, depth // 2
    return pl.pallas_call(
        base_kernel,
        in_specs=[SCALARS] + [THERE] * (len(pieces) + 1),
        out_specs=HERE,
        out_shape=jax.ShapeDtypeStruct((tokens, width), jnp.bfloat16),
        scratch_shapes=[
            pltpu.VMEM((len(pieces), rows, depth), jnp.bfloat16),
            pltpu.VMEM((2, *weight.shape[1:]), jnp.bfloat16),
            pltpu.SemaphoreType.DMA((len(pieces) + 2,)),
        ],
        compiler_params=pltpu.CompilerParams(vmem_limit_bytes=VMEM),
        cost_estimate=FREE,
        name="base",
    )(core, *pieces, weight)


def join_kernel(core, places, total, rest, own, other, weight, out, held, near, held_weight, made, sems, out_sems):
    blocks, rows, width = own.shape
    order = (0, 1, 2, 3, 6, 7, 4, 5)
    lies = [(part, i) for part in (total, rest) for i in range(part.shape[0] // rows)]
    pairs = [(weight.at[2], held_weight)]
    pairs += [
        (part.at[pl.ds(i * rows, rows)], held.at[places[b]]) for (part, i), b in zip(lies, order)
    ]
    for p in range(0, blocks, 2):
        pairs += [(part.at[p : p + 2], near.at[i, p : p + 2]) for i, part in enumerate((own, other))]
    copies = fetch(pairs, sems)
    for copy in copies[: 1 + blocks]:
        copy.wait()
    sent = []
    for p in range(0, blocks, 2):
        copies[1 + blocks + p].wait()
        copies[2 + blocks + p].wait()
        joined = dot(near[0, p : p + 2].reshape(2 * rows, width), held_weight[core[0]])
        joined += dot(near[1, p : p + 2].reshape(2 * rows, width), held_weight[1 - core[0]])
        joined = joined.reshape(2, rows, width) + held[p : p + 2].astype(jnp.float32)
        made[p : p + 2] = joined.astype(made.dtype)
        sent += fetch([(made.at[p : p + 2], out.at[p : p + 2])], out_sems.at[pl.ds(p // 2, 1)])
    for copy in sent:
        copy.wait()


def join(total, rest, own, other, weight, core, places):
    blocks, rows, width = own.shape
    return pl.pallas_call(
        join_kernel,
        in_specs=[SCALARS] * 2 + [THERE] * 5,
        out_specs=THERE,
        out_shape=jax.ShapeDtypeStruct(own.shape, own.dtype),
        scratch_shapes=[
            pltpu.VMEM(own.shape, own.dtype),
            pltpu.VMEM((2, *own.shape), own.dtype),
            pltpu.VMEM(weight.shape[1:], weight.dtype),
            pltpu.VMEM(own.shape, own.dtype),
            pltpu.SemaphoreType.DMA((1 + 2 * blocks,)),
            pltpu.SemaphoreType.DMA((blocks // 2,)),
        ],
        compiler_params=pltpu.CompilerParams(vmem_limit_bytes=VMEM),
        cost_estimate=FREE,
        name="join",
    )(core, places, total, rest, own, other, weight)


def grad_kernel(core, places, errors, *refs):
    count = len(refs) - 10
    boths, refs = refs[:count], refs[count:]
    top_own, top_other, out, near, ordered, held, tops, made, sems, out_sems = refs
    blocks, rows, width = errors.shape
    tokens = blocks * rows
    pairs = [(errors, near)]
    pairs += [(boths[i], held.at[0, i // 2]) for i in range(0, count, 2)]
    first = fetch(pairs, sems.at[pl.ds(0, len(pairs))])
    rest = [(boths[i], held.at[1, i // 2]) for i in range(1, count, 2)]
    rest += [(top_own, tops.at[0]), (top_other, tops.at[1])]
    first[0].wait()
    rest = fetch(rest, sems.at[pl.ds(len(pairs), len(rest))])
    for p in range(blocks):
        ordered[p * rows : (p + 1) * rows, :] = near[places[p]]
    for copy in first[1:]:
        copy.wait()
    sent = []
    for i in range(6):
        if i == 2:
            for copy in rest[: count // 2]:
                copy.wait()
        if i >= 4:
            rest[count // 2 + i - 4].wait()
        half = 1 - core[0] if i in (2, 3, 5) else core[0]
        for part in range(2):
            step, cut = 2 * i + part, width // 2
            slot = step % made.shape[0]
            if step >= made.shape[0]:
                sent[step - made.shape[0]].wait()
            if i < 4:
                begin = i % 2 * width + part * cut
                source = held[i // 2, :, :, begin : begin + cut].reshape(tokens, cut)
                against = ordered[...]
            else:
                source = tops[i - 4, :, part * cut : (part + 1) * cut]
                against = near[...].reshape(tokens, width)
            made[slot] = lax.dot_general(
                source, against, (((0,), (0,)), ((), ())), preferred_element_type=jnp.float32
            )
            target = out.at[i % 2 if i < 4 else 2, pl.ds(half * width + part * cut, cut)]
            copy = pltpu.make_async_copy(made.at[slot], target, out_sems.at[step])
            copy.start()
            sent.append(copy)
    for copy in sent[-made.shape[0] :]:
        copy.wait()


def grad(errors, boths, tops, core, places):
    blocks, rows, width = errors.shape
    tokens = blocks * rows
    count = len(boths)
    return pl.pallas_call(
        grad_kernel,
        in_specs=[SCALARS] * 2 + [THERE] * (count + 3),
        out_specs=THERE,
        out_shape=jax.ShapeDtypeStruct((3, 2 * width, width), jnp.float32),
        scratch_shapes=[
            pltpu.VMEM(errors.shape, jnp.bfloat16),
            pltpu.VMEM((tokens, width), jnp.bfloat16),
            pltpu.VMEM((2, count // 2, *boths[0].shape), jnp.bfloat16),
            pltpu.VMEM((2, tokens, width), jnp.bfloat16),
            pltpu.VMEM((4, width // 2, width), jnp.float32),
            pltpu.SemaphoreType.DMA((count + 3,)),
            pltpu.SemaphoreType.DMA((12,)),
        ],
        compiler_params=pltpu.CompilerParams(vmem_limit_bytes=VMEM),
        cost_estimate=FREE,
        name="grad",
    )(core, places, errors, *boths, *tops)


def local(
    queries,
    keys_cache,
    values_cache,
    prefix_len,
    accepted,
    residual_in,
    low_hidden,
    mid_hidden,
    out_weight,
    merge_weight,
):
    tokens, width = residual_in.shape
    me_dp, me_tp = lax.axis_index("dp"), lax.axis_index("tp")
    xl, z = me_dp // 4, me_dp % 4
    xh, y, core = me_tp // 8, me_tp // 2 % 4, me_tp % 2
    me = core.reshape(1)
    index = jnp.arange(CHIPS)
    held = ((xh ^ (index % 2)) * 4 + (z - y - index // 2) % 4).astype(jnp.int32)
    weight = merge_weight.reshape(3, 2, width, width)

    both = pack([low_hidden, mid_hidden], 1)
    both = [lax.ppermute(both, BOTH, way) for way in (TO_READER, TO_ACROSS)]
    context, taken = attend(
        queries, keys_cache[:, 0], values_cache[:, 0], prefix_len, out_weight, 1 - me
    )
    taken, *both = lax.optimization_barrier((taken, *both))
    both = pack(both, 0)
    both = [both] + [lax.ppermute(both, "tp", from_y(far)) for far in (1, 2, 3)]
    taken = lax.ppermute(taken, "tp", OTHER_CORE)
    kept = project(context, out_weight, me)
    pair = (kept.astype(jnp.float32) + taken.astype(jnp.float32)).astype(jnp.bfloat16)
    pair, both[1], both[3] = lax.optimization_barrier((pair, both[1], both[3]))
    parts = lax.all_to_all(pair, "tp", 0, 0, tiled=True, axis_index_groups=SAME_CORE)
    summed = jnp.sum(parts.astype(jnp.float32), axis=0)
    top_hidden = (residual_in.astype(jnp.float32) + summed).astype(jnp.bfloat16)

    def twins(pieces):
        return [half for piece in pieces for half in (piece, lax.ppermute(piece, "tp", OTHER_CORE))]

    first = twins([both[0], both[1], both[3]])
    total = base(first, weight, me)
    top_hidden, total, held = lax.optimization_barrier((top_hidden, total, held))

    top_moved = lax.ppermute(top_hidden, BOTH, TO_READER)
    second = twins([both[2]])
    rest = base(second, weight, me)
    top_own = spread(top_moved, BOTH, READERS)
    top_own, rest = lax.optimization_barrier((top_own, rest))
    top_other = lax.ppermute(top_own, "tp", OTHER_CORE)
    total = join(total, rest, top_own, top_other, weight, me, held)
    merged_parts = lax.all_to_all(total, "dp", 0, 0, tiled=True)
    merged = jnp.sum(merged_parts.astype(jnp.float32), axis=0)

    step = lax.broadcasted_iota(jnp.int32, (tokens, 1), 0) % STEPS
    keep = (step + 1 < jnp.repeat(accepted, STEPS)[:, None]).astype(jnp.float32)
    following = jnp.concatenate([top_hidden[1:], jnp.zeros_like(top_hidden[:1])], axis=0)
    following = jnp.where(step < STEPS - 1, following, jnp.zeros_like(following))
    scale = (CHIPS * tokens) ** (-0.5)
    errors = (keep * (merged - following.astype(jnp.float32)) * scale).astype(jnp.bfloat16)
    errors = spread(errors, "dp")

    boths = first[:4] + second + first[4:]
    tops = [part.reshape(CHIPS * tokens, width) for part in (top_own, top_other)]
    merge_grad = grad(errors, boths, tops, me, held)
    return (top_hidden, merge_grad)


def solution(mesh):
    in_specs = (
        P("dp", "tp"),
        P("dp", "tp", None, None),
        P("dp", "tp", None, None),
        P("dp"),
        P("dp"),
        P("dp", "tp"),
        P("dp", "tp"),
        P("dp", "tp"),
        P("tp", None),
        P(None, "dp", "tp"),
    )
    out_specs = (P("dp", "tp"), P(None, "dp", "tp"))
    return jax.shard_map(local, mesh=mesh, in_specs=in_specs, out_specs=out_specs, check_vma=False)
```

```python
import functools

import jax
import jax.numpy as jnp
from jax import lax
from jax.experimental import pallas as pl
from jax.experimental.pallas import tpu as pltpu
from jax.sharding import PartitionSpec as P

STEPS = 4
CHIPS = 8
VMEM = 61 * 2**20


def dev(xl, z, xh, y, c):
    return (xl * 4 + z) * 16 + xh * 8 + y * 2 + c


def coords():
    return [
        (xl, z, xh, y, c)
        for xl in range(2)
        for z in range(4)
        for xh in range(2)
        for y in range(4)
        for c in range(2)
    ]


TO_READER = [(dev(*p), dev(p[2], p[3], p[0], (p[3] - p[1]) % 4, p[4])) for p in coords()]
TO_ACROSS = [(dev(*p), dev(p[2], p[3], 1 - p[0], (p[3] - p[1]) % 4, p[4])) for p in coords()]
READERS = [
    [dev(xl, z, xh, (z - k) % 4, c) for xh in range(2) for k in range(4)]
    for xl in range(2)
    for z in range(4)
    for c in range(2)
]
SAME_CORE = [[2 * t + c for t in range(CHIPS)] for c in range(2)]
OTHER_CORE = [(j, j ^ 1) for j in range(16)]
BOTH = ("dp", "tp")
SCALARS = pl.BlockSpec(memory_space=pltpu.SMEM)
HERE = pl.BlockSpec(memory_space=pltpu.VMEM)
THERE = pl.BlockSpec(memory_space=pl.ANY)
FREE = pl.CostEstimate(flops=0, bytes_accessed=0, transcendentals=0)


def from_y(far):
    return [(j, (j & 8) | (j - 2 * far) % 8) for j in range(16)]


def dot(a, b):
    return jnp.dot(a, b, preferred_element_type=jnp.float32)


def spread(block, axis, groups=None):
    copies = jnp.broadcast_to(block[None], (CHIPS, *block.shape))
    return lax.all_to_all(copies, axis, 0, 0, tiled=True, axis_index_groups=groups)


def fetch(pairs, sems):
    copies = [
        pltpu.make_async_copy(source, target, sems.at[i])
        for i, (source, target) in enumerate(pairs)
    ]
    for copy in copies:
        copy.start()
    return copies


def attend_kernel(lens, half, queries, keys, values, weight, out, made, held, scores, weights, gathered, strips, sems, strip_sems):
    rows, width = held.shape[1], keys.shape[2]
    heads = queries.shape[1] // width
    size = heads * STEPS
    copies = fetch(
        [
            (source.at[pl.ds(i * rows // 2, rows // 2)], held.at[j, pl.ds(i * rows // 2, rows // 2)])
            for i in range(2)
            for j, source in enumerate((keys, values))
        ],
        sems,
    )
    cut = made.shape[-1]
    arriving = fetch(
        [
            (weight.at[:, pl.ds((2 * t + half[0]) * cut, cut)], strips.at[t])
            for t in range(CHIPS)
        ],
        strip_sems,
    )
    shape = (size, keys.shape[1])
    position = lax.broadcasted_iota(jnp.int32, shape, 1)
    step = lax.broadcasted_iota(jnp.int32, shape, 0) % STEPS
    scale = width ** (-0.5)
    for h in range(heads):
        asked = queries[:, h * width : (h + 1) * width].astype(jnp.float32)
        for r in range(rows):
            gathered[r, h * STEPS : (h + 1) * STEPS, :] = asked[r * STEPS : (r + 1) * STEPS]
    for i in range(2):
        copies[2 * i].wait()
        for r in range(i * rows // 2, (i + 1) * rows // 2):
            score = lax.dot_general(
                gathered[r].astype(queries.dtype), held[0, r], (((1,), (1,)), ((), ())), preferred_element_type=jnp.float32
            )
            visible = position < lens[r] + step + 1
            scores[r * size : (r + 1) * size, :] = jnp.where(visible, score * scale, -1e30)
        part = slice(i * rows * size // 2, (i + 1) * rows * size // 2)
        score = scores[part, :]
        expo = jnp.exp(score - jnp.max(score, axis=-1, keepdims=True))
        inverse = 1.0 / jnp.sum(expo, axis=-1, keepdims=True)
        weights[part, :] = (expo * inverse).astype(weights.dtype)
        copies[2 * i + 1].wait()
        for r in range(i * rows // 2, (i + 1) * rows // 2):
            gathered[r] = dot(weights[r * size : (r + 1) * size, :], held[1, r])
    for h in range(heads):
        context = [gathered[r, h * STEPS : (h + 1) * STEPS, :] for r in range(rows)]
        out[:, h * width : (h + 1) * width] = jnp.concatenate(context, axis=0).astype(out.dtype)
    for t in range(CHIPS):
        arriving[t].wait()
        made[t] = dot(out[...], strips[t]).astype(made.dtype)


def attend(queries, keys, values, lens, weight, half):
    rows, positions, width = keys.shape
    tokens, depth = queries.shape
    size = STEPS * depth // width
    cut = weight.shape[1] // (2 * CHIPS)
    return pl.pallas_call(
        attend_kernel,
        in_specs=[SCALARS, SCALARS, HERE, THERE, THERE, THERE],
        out_specs=[HERE, HERE],
        out_shape=[
            jax.ShapeDtypeStruct(queries.shape, queries.dtype),
            jax.ShapeDtypeStruct((CHIPS, tokens, cut), jnp.bfloat16),
        ],
        scratch_shapes=[
            pltpu.VMEM((2, rows, positions, width), jnp.bfloat16),
            pltpu.VMEM((rows * size, positions), jnp.float32),
            pltpu.VMEM((rows * size, positions), jnp.bfloat16),
            pltpu.VMEM((rows, size, width), jnp.float32),
            pltpu.VMEM((CHIPS, depth, cut), jnp.bfloat16),
            pltpu.SemaphoreType.DMA((4,)),
            pltpu.SemaphoreType.DMA((CHIPS,)),
        ],
        compiler_params=pltpu.CompilerParams(vmem_limit_bytes=VMEM),
        cost_estimate=FREE,
        name="attend",
    )(lens, half, queries, keys, values, weight)


def pack_kernel(cuts, *refs):
    *sources, out, held, in_sems, out_sem = refs
    for copy in fetch([(s, held.at[cut]) for s, cut in zip(sources, cuts)], in_sems):
        copy.wait()
    for copy in fetch([(held, out)], out_sem):
        copy.wait()


def pack(arrays, axis):
    shape = list(arrays[0].shape)
    size = shape[axis]
    cuts = [(slice(None),) * axis + (slice(i * size, (i + 1) * size),) for i in range(len(arrays))]
    shape[axis] *= len(arrays)
    return pl.pallas_call(
        functools.partial(pack_kernel, cuts),
        in_specs=[THERE] * len(arrays),
        out_specs=THERE,
        out_shape=jax.ShapeDtypeStruct(shape, arrays[0].dtype),
        scratch_shapes=[
            pltpu.VMEM(shape, arrays[0].dtype),
            pltpu.SemaphoreType.DMA((len(arrays),)),
            pltpu.SemaphoreType.DMA((1,)),
        ],
        compiler_params=pltpu.CompilerParams(vmem_limit_bytes=VMEM),
        cost_estimate=FREE,
        name="pack",
    )(*arrays)


def project_kernel(half, context, weight, out, held, sems):
    width = out.shape[-1]
    copies = fetch(
        [
            (weight.at[:, pl.ds((2 * t + half[0]) * width, width)], held.at[t])
            for t in range(CHIPS)
        ],
        sems,
    )
    for t in range(CHIPS):
        copies[t].wait()
        out[t] = dot(context[...], held[t]).astype(out.dtype)


def project(context, weight, half):
    tokens, depth = context.shape
    width = weight.shape[1] // (2 * CHIPS)
    return pl.pallas_call(
        project_kernel,
        in_specs=[SCALARS, HERE, THERE],
        out_specs=HERE,
        out_shape=jax.ShapeDtypeStruct((CHIPS, tokens, width), jnp.bfloat16),
        scratch_shapes=[
            pltpu.VMEM((CHIPS, depth, width), jnp.bfloat16),
            pltpu.SemaphoreType.DMA((CHIPS,)),
        ],
        compiler_params=pltpu.CompilerParams(vmem_limit_bytes=VMEM),
        cost_estimate=FREE,
        name="project",
    )(half, context, weight)


def base_kernel(core, *refs):
    count = len(refs) - 5
    sources, (weight, out, held, held_weight, sems) = refs[:count], refs[count:]
    copies = fetch(
        [(weight.at[k], held_weight.at[k]) for k in range(2)]
        + [(source, held.at[i]) for i, source in enumerate(sources)],
        sems,
    )
    half = core[0]
    width = out.shape[-1]
    rows = sources[0].shape[0]
    copies[0].wait()
    copies[1].wait()
    for i in range(count // 2):
        copies[2 + 2 * i].wait()
        copies[3 + 2 * i].wait()
        total = dot(held[2 * i, :, :width], held_weight[0, half])
        total += dot(held[2 * i, :, width:], held_weight[1, half])
        total += dot(held[2 * i + 1, :, :width], held_weight[0, 1 - half])
        total += dot(held[2 * i + 1, :, width:], held_weight[1, 1 - half])
        out[i * rows : (i + 1) * rows, :] = total.astype(out.dtype)


def base(pieces, weight, core):
    rows, depth = pieces[0].shape
    tokens, width = len(pieces) // 2 * rows, depth // 2
    return pl.pallas_call(
        base_kernel,
        in_specs=[SCALARS] + [THERE] * (len(pieces) + 1),
        out_specs=HERE,
        out_shape=jax.ShapeDtypeStruct((tokens, width), jnp.bfloat16),
        scratch_shapes=[
            pltpu.VMEM((len(pieces), rows, depth), jnp.bfloat16),
            pltpu.VMEM((2, *weight.shape[1:]), jnp.bfloat16),
            pltpu.SemaphoreType.DMA((len(pieces) + 2,)),
        ],
        compiler_params=pltpu.CompilerParams(vmem_limit_bytes=VMEM),
        cost_estimate=FREE,
        name="base",
    )(core, *pieces, weight)


def join_kernel(core, places, total, rest, own, other, weight, out, held, near, held_weight, made, sems, out_sems):
    blocks, rows, width = own.shape
    order = (0, 1, 2, 3, 6, 7, 4, 5)
    lies = [(part, i) for part in (total, rest) for i in range(part.shape[0] // rows)]
    pairs = [(weight.at[2], held_weight)]
    pairs += [
        (part.at[pl.ds(i * rows, rows)], held.at[places[b]]) for (part, i), b in zip(lies, order)
    ]
    for p in range(0, blocks, 4):
        pairs += [(part.at[p : p + 4], near.at[i, p : p + 4]) for i, part in enumerate((own, other))]
    copies = fetch(pairs, sems.at[pl.ds(0, len(pairs))])
    for copy in copies[: 1 + blocks]:
        copy.wait()
    sent = []
    for p in range(0, blocks, 4):
        copies[1 + blocks + p // 2].wait()
        copies[2 + blocks + p // 2].wait()
        joined = dot(near[0, p : p + 4].reshape(4 * rows, width), held_weight[core[0]])
        joined += dot(near[1, p : p + 4].reshape(4 * rows, width), held_weight[1 - core[0]])
        joined = joined.reshape(4, rows, width) + held[p : p + 4].astype(jnp.float32)
        made[p : p + 4] = joined.astype(made.dtype)
        sent += fetch([(made.at[p : p + 4], out.at[p : p + 4])], out_sems.at[pl.ds(p // 4, 1)])
    for copy in sent:
        copy.wait()


def join(total, rest, own, other, weight, core, places):
    blocks, rows, width = own.shape
    return pl.pallas_call(
        join_kernel,
        in_specs=[SCALARS] * 2 + [THERE] * 5,
        out_specs=THERE,
        out_shape=jax.ShapeDtypeStruct(own.shape, own.dtype),
        scratch_shapes=[
            pltpu.VMEM(own.shape, own.dtype),
            pltpu.VMEM((2, *own.shape), own.dtype),
            pltpu.VMEM(weight.shape[1:], weight.dtype),
            pltpu.VMEM(own.shape, own.dtype),
            pltpu.SemaphoreType.DMA((1 + 2 * blocks,)),
            pltpu.SemaphoreType.DMA((blocks // 2,)),
        ],
        compiler_params=pltpu.CompilerParams(vmem_limit_bytes=VMEM),
        cost_estimate=FREE,
        name="join",
    )(core, places, total, rest, own, other, weight)


def grad_kernel(core, places, errors, *refs):
    count = len(refs) - 10
    boths, refs = refs[:count], refs[count:]
    top_own, top_other, out, near, ordered, held, tops, made, sems, out_sems = refs
    blocks, rows, width = errors.shape
    tokens = blocks * rows
    pairs = [(errors, near)]
    pairs += [(boths[i], held.at[0, i // 2]) for i in range(0, count, 2)]
    first = fetch(pairs, sems.at[pl.ds(0, len(pairs))])
    rest = [(boths[i], held.at[1, i // 2]) for i in range(1, count, 2)]
    rest += [(top_own, tops.at[0]), (top_other, tops.at[1])]
    first[0].wait()
    rest = fetch(rest, sems.at[pl.ds(len(pairs), len(rest))])
    for p in range(blocks):
        ordered[p * rows : (p + 1) * rows, :] = near[places[p]]
    for copy in first[1:]:
        copy.wait()
    sent = []
    for i in range(6):
        if i == 2:
            for copy in rest[: count // 2]:
                copy.wait()
        if i >= 4:
            rest[count // 2 + i - 4].wait()
        half = 1 - core[0] if i in (2, 3, 5) else core[0]
        for part in range(2):
            step, cut = 2 * i + part, width // 2
            slot = step % made.shape[0]
            if step >= made.shape[0]:
                sent[step - made.shape[0]].wait()
            if i < 4:
                begin = i % 2 * width + part * cut
                source = held[i // 2, :, :, begin : begin + cut].reshape(tokens, cut)
                against = ordered[...]
            else:
                source = tops[i - 4, :, part * cut : (part + 1) * cut]
                against = near[...].reshape(tokens, width)
            made[slot] = lax.dot_general(
                source, against, (((0,), (0,)), ((), ())), preferred_element_type=jnp.float32
            )
            target = out.at[i % 2 if i < 4 else 2, pl.ds(half * width + part * cut, cut)]
            copy = pltpu.make_async_copy(made.at[slot], target, out_sems.at[step])
            copy.start()
            sent.append(copy)
    for copy in sent[-made.shape[0] :]:
        copy.wait()


def grad(errors, boths, tops, core, places):
    blocks, rows, width = errors.shape
    tokens = blocks * rows
    count = len(boths)
    return pl.pallas_call(
        grad_kernel,
        in_specs=[SCALARS] * 2 + [THERE] * (count + 3),
        out_specs=THERE,
        out_shape=jax.ShapeDtypeStruct((3, 2 * width, width), jnp.float32),
        scratch_shapes=[
            pltpu.VMEM(errors.shape, jnp.bfloat16),
            pltpu.VMEM((tokens, width), jnp.bfloat16),
            pltpu.VMEM((2, count // 2, *boths[0].shape), jnp.bfloat16),
            pltpu.VMEM((2, tokens, width), jnp.bfloat16),
            pltpu.VMEM((4, width // 2, width), jnp.float32),
            pltpu.SemaphoreType.DMA((count + 3,)),
            pltpu.SemaphoreType.DMA((12,)),
        ],
        compiler_params=pltpu.CompilerParams(vmem_limit_bytes=VMEM),
        cost_estimate=FREE,
        name="grad",
    )(core, places, errors, *boths, *tops)


def local(
    queries,
    keys_cache,
    values_cache,
    prefix_len,
    accepted,
    residual_in,
    low_hidden,
    mid_hidden,
    out_weight,
    merge_weight,
):
    tokens, width = residual_in.shape
    me_dp, me_tp = lax.axis_index("dp"), lax.axis_index("tp")
    xl, z = me_dp // 4, me_dp % 4
    xh, y, core = me_tp // 8, me_tp // 2 % 4, me_tp % 2
    me = core.reshape(1)
    index = jnp.arange(CHIPS)
    held = ((xh ^ (index % 2)) * 4 + (z - y - index // 2) % 4).astype(jnp.int32)
    weight = merge_weight.reshape(3, 2, width, width)

    both = pack([low_hidden, mid_hidden], 1)
    both = [lax.ppermute(both, BOTH, way) for way in (TO_READER, TO_ACROSS)]
    context, taken = attend(
        queries, keys_cache[:, 0], values_cache[:, 0], prefix_len, out_weight, 1 - me
    )
    taken, *both = lax.optimization_barrier((taken, *both))
    both = pack(both, 0)
    both = [both] + [lax.ppermute(both, "tp", from_y(far)) for far in (1, 2, 3)]
    taken = lax.ppermute(taken, "tp", OTHER_CORE)
    kept = project(context, out_weight, me)
    pair = (kept.astype(jnp.float32) + taken.astype(jnp.float32)).astype(jnp.bfloat16)
    pair, both[1], both[3] = lax.optimization_barrier((pair, both[1], both[3]))
    parts = lax.all_to_all(pair, "tp", 0, 0, tiled=True, axis_index_groups=SAME_CORE)
    summed = jnp.sum(parts.astype(jnp.float32), axis=0)
    top_hidden = (residual_in.astype(jnp.float32) + summed).astype(jnp.bfloat16)

    def twins(pieces):
        return [half for piece in pieces for half in (piece, lax.ppermute(piece, "tp", OTHER_CORE))]

    first = twins([both[0], both[1], both[3]])
    total = base(first, weight, me)
    top_hidden, total, held = lax.optimization_barrier((top_hidden, total, held))

    top_moved = lax.ppermute(top_hidden, BOTH, TO_READER)
    second = twins([both[2]])
    rest = base(second, weight, me)
    top_own = spread(top_moved, BOTH, READERS)
    top_own, rest = lax.optimization_barrier((top_own, rest))
    top_other = lax.ppermute(top_own, "tp", OTHER_CORE)
    total = join(total, rest, top_own, top_other, weight, me, held)
    merged_parts = lax.all_to_all(total, "dp", 0, 0, tiled=True)
    merged = jnp.sum(merged_parts.astype(jnp.float32), axis=0)

    step = lax.broadcasted_iota(jnp.int32, (tokens, 1), 0) % STEPS
    keep = (step + 1 < jnp.repeat(accepted, STEPS)[:, None]).astype(jnp.float32)
    following = jnp.concatenate([top_hidden[1:], jnp.zeros_like(top_hidden[:1])], axis=0)
    following = jnp.where(step < STEPS - 1, following, jnp.zeros_like(following))
    scale = (CHIPS * tokens) ** (-0.5)
    errors = (keep * (merged - following.astype(jnp.float32)) * scale).astype(jnp.bfloat16)
    errors = spread(errors, "dp")

    boths = first[:4] + second + first[4:]
    tops = [part.reshape(CHIPS * tokens, width) for part in (top_own, top_other)]
    merge_grad = grad(errors, boths, tops, me, held)
    return (top_hidden, merge_grad)


def solution(mesh):
    in_specs = (
        P("dp", "tp"),
        P("dp", "tp", None, None),
        P("dp", "tp", None, None),
        P("dp"),
        P("dp"),
        P("dp", "tp"),
        P("dp", "tp"),
        P("dp", "tp"),
        P("tp", None),
        P(None, "dp", "tp"),
    )
    out_specs = (P("dp", "tp"), P(None, "dp", "tp"))
    return jax.shard_map(local, mesh=mesh, in_specs=in_specs, out_specs=out_specs, check_vma=False)
```
